32 devices in a mesh: member: 2 (over y), lon: 8 (over z, x), lat: 2 (over core).
Axes of the slice: x: 2, y: 2, z: 4, core: 2. Of those that a mesh axis runs over, the one named last changes fastest.
Arguments:
- state: float32 [8, 32, 128, 256], P(('member', 'lat'), 'lon'), parts along dimension 0, may hold values from -4 to 4
- weights: bfloat16 [4, 4, 32, 6, 128, 128], P(None, 'lat', 'lon'), may hold values from -0.21875 to 0.21875
- positions: float32 [3, 4, 32, 128], P(None, 'lat', 'lon'), may hold values from -1 to 1
- stencil_codes: int32 [4, 32, 6], P('lat', 'lon'), may hold values from 0 to 8, as said below
- ovl_owner: int32 [512, 2, 1], P(('lon', 'lat')), may hold values from 0 to 15, as said below
- ovl_local: int32 [512, 2], P(('lon', 'lat')), may hold values from 0 to 7
- interp: bfloat16 [512, 2, 128, 128], P(('lon', 'lat')), may hold values from -0.375 to 0.375
Outputs:
- next_state: float32 [8, 32, 128, 256], P(('member', 'lat'), 'lon'), parts along dimension 0
- ocean: bfloat16 [1024, 128, 256], P(('member', 'lon', 'lat')), parts along dimension 0
The draws below stay inside these ranges and needn't reach their ends.
There are 2 independent parts, one for each index of `member`. The reference program is written for one: setup_inputs(seed, part) draws one part's arguments, and reference() takes and returns one part's arrays. A program takes and returns all parts, laid end to end along the dimension named above; an argument that names none is the same for every part. Nothing has to cross between parts.
Inputs may be any that keep to these rules, and one draw needn't show every extreme that they name: `stencil_codes`: each row tile's codes are distinct, include 4 (the tile itself), and never point outside the latitude range. `ovl_owner`: the owners named in the rows of the device with longitude index l lie in sector (l + 4) mod 8 or the two beside it, in any latitude band; among the rows of one device no owner is named more than 16 times, and the owner in the device's own band and that centre sector exactly 16 times.
All inputs are finite; a program needn't handle non-finite values.
Results may differ from the reference program's by a relative error of at most 0.0051.
Values may be sent and summed in bfloat16 or wider, within the bound.
No kernel may reach another device: no remote copies, remote signals or barrier semaphores. Data moves between devices by JAX's collectives and lax.ppermute only.
A program may use at most 64 MiB of HBM per device.

```python
import jax
import jax.numpy as jnp
from jax import lax

TILE_NODES = 128
STENCIL_TILES = 6
INTERSECTIONS = 2
LAT_TILES = 2
LON_TILES = 4
OCEAN_DEV = 32
FEATURES = 256
LAT_TOTAL = 4
LON_TOTAL = 32
OWNERS = 16
OCEAN_TILES = 512
CAPACITY = 16
N_LON = 8
N_LAT = 2


def draw_positions(key, part):
    key = jax.random.fold_in(key, 7)
    raw_vectors = jax.random.normal(key, (3, LAT_TOTAL, LON_TOTAL, TILE_NODES), jnp.float32)
    length = jnp.sqrt(jnp.sum(raw_vectors * raw_vectors, axis=0, keepdims=True) + 1e-06)
    return raw_vectors / length


def draw_stencil_codes(key, part):
    key = jax.random.fold_in(key, 11)
    raw_scores = jax.random.randint(key, (LAT_TOTAL, LON_TOTAL, 9), 0, 1 << 20)
    code_iota = lax.broadcasted_iota(jnp.int32, (LAT_TOTAL, LON_TOTAL, 9), 2)
    row_iota = lax.broadcasted_iota(jnp.int32, (LAT_TOTAL, LON_TOTAL, 9), 0)
    scores = raw_scores * 16 + code_iota
    lat_offset = code_iota // 3 - 1
    outside = (row_iota == 0) & (lat_offset == -1) | (row_iota == LAT_TOTAL - 1) & (lat_offset == 1)
    scores = jnp.where(outside, -1, scores)
    scores = jnp.where(code_iota == 4, 1 << 26, scores)
    chosen_scores, chosen = lax.top_k(scores, STENCIL_TILES)
    return chosen.astype(jnp.int32)


def draw_ovl_owner(key, part):
    key = jax.random.fold_in(key, 13)
    row_count = OCEAN_DEV * INTERSECTIONS
    window = 3 * N_LAT
    spare = (window - 1) * CAPACITY
    slot_iota = lax.broadcasted_iota(jnp.int32, (OWNERS, spare), 1)
    scores = jax.random.randint(key, (OWNERS, spare), 0, 1 << 20) * spare + slot_iota
    order = jnp.argsort(scores, axis=1).astype(jnp.int32)
    picked = order[:, :row_count - CAPACITY] // CAPACITY
    device = lax.broadcasted_iota(jnp.int32, (OWNERS, 1), 0)
    dev_lon = device // N_LAT
    dev_lat = device % N_LAT
    own_slot = N_LAT + dev_lat
    others = picked + (picked >= own_slot).astype(jnp.int32)
    forced = jnp.broadcast_to(own_slot, (OWNERS, CAPACITY))
    slots = jnp.concatenate([forced, others], axis=1)
    center = (dev_lon + N_LON // 2) % N_LON
    owner_lon = (center - 1 + N_LON + slots // N_LAT) % N_LON
    owner = owner_lon * N_LAT + slots % N_LAT
    return owner.reshape(OCEAN_TILES, INTERSECTIONS, 1).astype(jnp.int32)


def place_ends(values, key, smallest, high):
    shape = values.shape
    place = [jax.random.randint(jax.random.fold_in(key, axis), (), 0, shape[axis]) for axis in range(len(shape))]
    values = values.at[tuple(place)].set(smallest)
    longest = shape.index(max(shape))
    place[longest] = (place[longest] + 1) % shape[longest]
    return values.at[tuple(place)].set(high)


def steps_of(own_key, dims, cuts, smallest, high):
    level = 1.0
    for position, shards_of in cuts:
        heights = jax.random.uniform(jax.random.fold_in(jax.random.fold_in(own_key, 6), position), (shards_of,), jnp.float32, smallest / len(cuts), high / len(cuts))
        level = level * jnp.repeat(jnp.exp(heights), dims[position] // shards_of).reshape((-1,) + (1,) * (len(dims) - 1 - position))
    return level


def scatter_about(stream_key, dims, deviation, limit, split=(), kind=jnp.bfloat16):
    drawn = jax.random.normal(stream_key, dims, jnp.float32) * deviation
    if len(split) > 0:
        drawn = steps_of(stream_key, dims, split, -0.22, 0.18) * drawn
    return jnp.clip(drawn, min=-limit, max=limit).astype(kind)


def setup_inputs(seed: int = 0, part: int = 0) -> dict:
    key_of = jax.random.split(jax.random.key(seed), 8)
    own_keys = jax.random.split(jax.random.fold_in(key_of[7], part), 8)
    state = scatter_about(own_keys[0], (LAT_TOTAL, LON_TOTAL, TILE_NODES, FEATURES), 1.0, 4.0, ((0, 2), (1, 8)), jnp.float32)
    weights = scatter_about(key_of[1], (4, LAT_TOTAL, LON_TOTAL, STENCIL_TILES, TILE_NODES, TILE_NODES), (STENCIL_TILES * TILE_NODES) ** -0.5, 0.21875, ((1, 2), (2, 8)))
    positions = draw_positions(jax.random.fold_in(key_of[7], 71), part)
    stencil_codes = draw_stencil_codes(jax.random.fold_in(key_of[7], 71), part)
    ovl_owner = draw_ovl_owner(jax.random.fold_in(key_of[7], 71), part)
    ovl_local = place_ends(jax.random.randint(key_of[5], (OCEAN_TILES, INTERSECTIONS), 0, LAT_TILES * LON_TILES), jax.random.fold_in(key_of[5], 1), 0, (LAT_TILES * LON_TILES) - 1).astype(jnp.int32)
    interp = scatter_about(key_of[6], (OCEAN_TILES, INTERSECTIONS, TILE_NODES, TILE_NODES), (INTERSECTIONS * TILE_NODES) ** -0.5, 0.375, ((0, 16),))
    return dict(state=state, weights=weights, positions=positions, stencil_codes=stencil_codes, ovl_owner=ovl_owner, ovl_local=ovl_local, interp=interp)


GRAVITY = 1.0
CORIOLIS = 2.0
STEP_SIZE = 0.2


def tendency_from(current, derivs, positions):
    split_shape = current.shape[:-1] + (4, current.shape[-1] // 4)
    fields = current.reshape(split_shape)
    grads = derivs.reshape((4,) + split_shape)
    coords = [positions[component][..., None] for component in range(3)]
    velocity = [fields[..., component, :] for component in range(3)]
    height = fields[..., 3, :]
    rotation = CORIOLIS * coords[2]
    cross = [coords[1] * velocity[2] - coords[2] * velocity[1],
             coords[2] * velocity[0] - coords[0] * velocity[2],
             coords[0] * velocity[1] - coords[1] * velocity[0]]
    forcing = []
    for component in range(3):
        advect = (velocity[0] * grads[0][..., component, :] + velocity[1] * grads[1][..., component, :]
                  + velocity[2] * grads[2][..., component, :])
        forcing.append(-advect - rotation * cross[component] - GRAVITY * grads[component][..., 3, :]
                       + grads[3][..., component, :])
    radial = coords[0] * forcing[0] + coords[1] * forcing[1] + coords[2] * forcing[2]
    moment = [forcing[component] - coords[component] * radial for component in range(3)]
    diverge = grads[0][..., 0, :] + grads[1][..., 1, :] + grads[2][..., 2, :]
    height_rate = -(velocity[0] * grads[0][..., 3, :] + velocity[1] * grads[1][..., 3, :]
                    + velocity[2] * grads[2][..., 3, :]) - height * diverge + grads[3][..., 3, :]
    return jnp.stack(moment + [height_rate], axis=-2).reshape(current.shape)


def neighbor_terms(rounded, weights, stencil_codes):
    lat_total, lon_total = rounded.shape[0], rounded.shape[1]
    wrapped = jnp.concatenate([rounded[:, -1:], rounded, rounded[:, :1]], axis=1)
    padded = jnp.pad(wrapped, ((1, 1), (0, 0), (0, 0), (0, 0)))
    lon_iota = jnp.arange(lon_total, dtype=jnp.int32)

    def one_row(lat_row):
        codes = stencil_codes[lat_row]
        row_index = (lat_row + codes // 3).astype(jnp.int32)
        col_index = (lon_iota[:, None] + codes % 3).astype(jnp.int32)
        nearby = padded[row_index, col_index]
        weight_row = weights[:, lat_row]
        return jnp.einsum("qbkij,bkjf->qbif", weight_row.astype(jnp.float32), nearby.astype(jnp.float32))

    terms = lax.map(one_row, jnp.arange(lat_total, dtype=jnp.int32))
    return jnp.moveaxis(terms, 0, 1)


def reference(state, weights, positions, stencil_codes, ovl_owner, ovl_local, interp):
    def rate(current):
        rounded = current.astype(jnp.bfloat16)
        return tendency_from(current, neighbor_terms(rounded, weights, stencil_codes), positions)

    first = rate(state)
    second = rate(state + 0.5 * STEP_SIZE * first)
    third = rate(state + 0.5 * STEP_SIZE * second)
    fourth = rate(state + STEP_SIZE * third)
    next_state = state + (STEP_SIZE / 6.0) * (first + 2.0 * second + 2.0 * third + fourth)
    final = next_state.astype(jnp.bfloat16)
    owners = ovl_owner[..., 0]
    lat_tile = ((owners % N_LAT) * LAT_TILES + ovl_local // LON_TILES).astype(jnp.int32)
    lon_tile = ((owners // N_LAT) * LON_TILES + ovl_local % LON_TILES).astype(jnp.int32)
    lat_blocks = lat_tile.reshape(OWNERS, OCEAN_DEV, INTERSECTIONS)
    lon_blocks = lon_tile.reshape(OWNERS, OCEAN_DEV, INTERSECTIONS)
    interp_blocks = interp.reshape(OWNERS, OCEAN_DEV, INTERSECTIONS, TILE_NODES, TILE_NODES)

    def one_block(pieces):
        lat_block, lon_block, interp_block = pieces
        nearby = final[lat_block, lon_block]
        mixed = jnp.einsum("ojst,ojsf->otf", interp_block.astype(jnp.float32), nearby.astype(jnp.float32))
        return mixed.astype(jnp.bfloat16)

    ocean = lax.map(one_block, (lat_blocks, lon_blocks, interp_blocks))
    ocean = ocean.reshape(OCEAN_TILES, TILE_NODES, FEATURES)
    return next_state, ocean
```

```python
import functools

import jax
import jax.numpy as jnp
from jax import lax
from jax.experimental import pallas as pl
from jax.experimental.pallas import tpu as pltpu
from jax.sharding import PartitionSpec as P

CORIOLIS = 2.0
STEP_SIZE = 0.2
BF16 = jnp.bfloat16
F32 = jnp.float32
ANY = pl.BlockSpec(memory_space=pl.ANY)
VMEM = pl.BlockSpec(memory_space=pltpu.VMEM)
SMEM = pl.BlockSpec(memory_space=pltpu.SMEM)
LIMIT = 48 * 1024 * 1024


def in_vmem(value):
    return pltpu.with_memory_space_constraint(value, pltpu.VMEM)


def prep_kernel(send_ref, state_ref, pos_ref, own_ref, west_ref, east_ref, row_ref, coef_ref):
    rows, cols = state_ref.shape[:2]
    for a in range(rows):
        for b in range(cols):
            tile = state_ref[a, b].astype(BF16)
            own_ref[a, b] = tile
            if b == 0:
                west_ref[a, 0] = tile
            if b == cols - 1:
                east_ref[a, 0] = tile

            @pl.when(send_ref[0] == a)
            def _():
                row_ref[0, b] = tile

    nodes = pos_ref.shape[-1]
    low = lax.broadcasted_iota(jnp.int32, (nodes, nodes), 1) < nodes // 2
    for a in range(rows):
        for b in range(cols):
            x0, x1, x2 = (
                jnp.broadcast_to(pos_ref[c, a, b][None, :], (nodes, nodes)).T for c in range(3)
            )
            spin = CORIOLIS * x2
            coef_ref[a, b, 0] = jnp.where(low, x0, x1)
            coef_ref[a, b, 1] = jnp.where(low, x2, 0.0)
            coef_ref[a, b, 2] = spin * jnp.where(low, x1, -x0)
            coef_ref[a, b, 3] = spin * jnp.where(low, -x2, x2)
            coef_ref[a, b, 4] = jnp.where(low, spin * x0, 0.0)
            coef_ref[a, b, 5] = jnp.where(low, spin * x1, 0.0)


def turned(value):
    return pltpu.roll(value, value.shape[-1] // 2, axis=1)


def tendency(tile, grads, coef, low):
    half = tile.shape[-1] // 2
    sa, sb = tile[:, :half], tile[:, half:]
    ra, rb = turned(sa), turned(sb)
    v0 = jnp.where(low, sa, ra)
    v1 = jnp.where(low, ra, sa)
    v2 = jnp.where(low, sb, rb)
    ga = [g[:, :half] for g in grads]
    gb = [g[:, half:] for g in grads]
    t0a, t0b, t2b = turned(ga[0]), turned(gb[0]), turned(gb[2])
    fa = (
        ga[3]
        - (v0 * ga[0] + v1 * ga[1] + v2 * ga[2])
        - (coef[2] * v2 + coef[3] * ra)
        - jnp.where(low, t0b, gb[1])
    )
    spread = sb * (t0a + ga[1] + t2b)
    fb = (
        gb[3]
        - (v0 * gb[0] + v1 * gb[1] + v2 * gb[2])
        - (coef[4] * v1 - coef[5] * v0)
        - jnp.where(low, t2b, spread)
    )
    part = coef[0] * fa + coef[1] * fb
    radial = part + turned(part)
    return fa - coef[0] * radial, fb - coef[1] * radial


def stage_kernel(last, scale, index_ref, send_ref, w_ref, coef_ref, *refs):
    if last:
        (state_ref, second_ref, third_ref, now_ref, own_ref, west_ref, east_ref, other_ref,
         cwest_ref, ceast_ref, next_ref, bown_ref, ext, sems) = refs
    else:
        (state_ref, now_ref, own_ref, west_ref, east_ref, other_ref,
         cwest_ref, ceast_ref, next_ref, bown_ref, bwest_ref, beast_ref, brow_ref, ext, sems) = refs
    rows, cols, nodes, feats = state_ref.shape
    mine = 1 - send_ref[0]
    copies = [
        pltpu.make_async_copy(own_ref, ext.at[0:rows, 1 : cols + 1], sems.at[0]),
        pltpu.make_async_copy(west_ref, ext.at[0:rows, 0:1], sems.at[1]),
        pltpu.make_async_copy(east_ref, ext.at[0:rows, cols + 1 : cols + 2], sems.at[2]),
        pltpu.make_async_copy(other_ref, ext.at[rows : rows + 1, 1 : cols + 1], sems.at[3]),
        pltpu.make_async_copy(
            cwest_ref.at[pl.ds(mine, 1)], ext.at[rows : rows + 1, 0:1], sems.at[4]
        ),
        pltpu.make_async_copy(
            ceast_ref.at[pl.ds(mine, 1)], ext.at[rows : rows + 1, cols + 1 : cols + 2], sems.at[5]
        ),
    ]
    for copy in copies:
        copy.start()
    for copy in copies:
        copy.wait()
    low = lax.broadcasted_iota(jnp.int32, (nodes, feats // 2), 1) < feats // 4
    half = feats // 2
    taps = w_ref.shape[3]
    for a in range(rows):
        for b in range(cols):
            where = [index_ref[a, b, k] for k in range(taps)]
            near = jnp.concatenate(
                [ext[w // (cols + 2), w % (cols + 2)] for w in where], axis=0
            )
            weights = jnp.concatenate(
                [
                    jnp.concatenate([w_ref[q, a, b, k] for k in range(taps)], axis=1)
                    for q in range(4)
                ],
                axis=0,
            )
            derivs = jnp.dot(weights, near, preferred_element_type=F32)
            grads = [derivs[q * nodes : (q + 1) * nodes] for q in range(4)]
            coef = [coef_ref[a, b, i] for i in range(6)]
            ka, kb = tendency(now_ref[a, b], grads, coef, low)
            rate = jnp.concatenate([ka, kb], axis=1)
            if last:
                third = 1.0 / 3.0
                out = (
                    third * (second_ref[a, b] + 2.0 * third_ref[a, b] + now_ref[a, b] - state_ref[a, b])
                    + scale * rate
                )
            else:
                out = state_ref[a, b] + scale * rate
            next_ref[a, b] = out
            rounded = out.astype(BF16)
            bown_ref[a, b] = rounded
            if not last:
                if b == 0:
                    bwest_ref[a, 0] = rounded
                if b == cols - 1:
                    beast_ref[a, 0] = rounded

                @pl.when(send_ref[0] == a)
                def _():
                    brow_ref[0, b] = rounded


def turn_kernel(interp_ref, out_ref):
    tiles, taps, nodes, points = interp_ref.shape
    for o in range(tiles):
        out_ref[o] = interp_ref[o].reshape(taps * nodes, points).T


def ocean_kernel(slot_ref, ends_ref, interp_ref, *refs):
    *sources, nat_ref, other_nat_ref, out_ref, tiles, sems = refs
    count = sources[0].shape[0]

    def copy(source, place):
        return pltpu.make_async_copy(source, tiles.at[place], sems.at[place])

    plain = (ends_ref[0] == 0, None, ends_ref[1] == 0)

    @pl.when(pl.program_id(0) == 0)
    def _():
        for place in range(6):
            use = plain[place // 2]
            if use is None:
                copy(sources[place], place).start()
            else:
                nat = (nat_ref, other_nat_ref)[place % 2]

                @pl.when(use)
                def _():
                    copy(sources[place], place).start()

                @pl.when(jnp.logical_not(use))
                def _():
                    copy(nat, place).start()

        for place in range(6):
            copy(sources[place], place).wait()

    block, taps = interp_ref.shape[0], slot_ref.shape[1]
    base = pl.program_id(0) * block
    for o in range(block):
        where = [slot_ref[base + o, j] for j in range(taps)]
        near = jnp.concatenate([tiles[w // count, w % count] for w in where], axis=0)
        out_ref[o] = jnp.dot(interp_ref[o], near, preferred_element_type=F32).astype(BF16)


def local(state, weights, positions, stencil_codes, ovl_owner, ovl_local, interp):
    rows, cols, nodes, feats = state.shape
    taps = stencil_codes.shape[-1]
    lon_count = lax.axis_size("lon")
    lat_count = lax.axis_size("lat")
    my_lon = lax.axis_index("lon")
    my_lat = lax.axis_index("lat")
    forward = [(i, (i + 1) % lon_count) for i in range(lon_count)]
    backward = [(target, source) for source, target in forward]
    swap = [(i, lat_count - 1 - i) for i in range(lat_count)]
    params = pltpu.CompilerParams(vmem_limit_bytes=LIMIT)

    tile_row = lax.broadcasted_iota(jnp.int32, stencil_codes.shape, 0)
    tile_col = lax.broadcasted_iota(jnp.int32, stencil_codes.shape, 1)
    ext_row = tile_row + stencil_codes // 3 - 1
    ext_row = jnp.where(ext_row < 0, rows, ext_row)
    index = ext_row * (cols + 2) + tile_col + stencil_codes % 3
    send = (1 - my_lat).astype(jnp.int32).reshape(1)

    col_shape = (rows, 1, nodes, feats)
    row_shape = (1, cols, nodes, feats)
    bf_shapes = [
        jax.ShapeDtypeStruct((rows, cols, nodes, feats), BF16),
        jax.ShapeDtypeStruct(col_shape, BF16),
        jax.ShapeDtypeStruct(col_shape, BF16),
        jax.ShapeDtypeStruct(row_shape, BF16),
    ]
    own, west, east, row, coef = pl.pallas_call(
        prep_kernel,
        out_shape=bf_shapes + [jax.ShapeDtypeStruct((rows, cols, 6, nodes, nodes), F32)],
        in_specs=[SMEM, VMEM, VMEM],
        out_specs=[VMEM] * 5,
        compiler_params=params,
        name="prep",
    )(send, state, positions)

    def halo(west, east, row):
        from_west = lax.ppermute(east, "lon", forward)
        from_east = lax.ppermute(west, "lon", backward)
        other = lax.ppermute(row, "lat", swap)
        corner_west = lax.ppermute(from_west, "lat", swap)
        corner_east = lax.ppermute(from_east, "lat", swap)
        return from_west, from_east, other, corner_west, corner_east

    flops = 2 * 4 * rows * cols * taps * nodes * nodes * feats

    def stage(scale, fields, own, edges, last=False):
        outs = [pltpu.VMEM((rows, cols, nodes, feats), F32)] if False else [
            jax.ShapeDtypeStruct((rows, cols, nodes, feats), F32)
        ]
        outs = outs + (bf_shapes[:1] if last else bf_shapes)
        return pl.pallas_call(
            functools.partial(stage_kernel, last, scale),
            out_shape=outs,
            in_specs=[SMEM, SMEM, VMEM, VMEM] + [VMEM] * len(fields) + [ANY] * 6,
            out_specs=[VMEM] * len(outs),
            scratch_shapes=[
                pltpu.VMEM((rows + 1, cols + 2, nodes, feats), BF16),
                pltpu.SemaphoreType.DMA((6,)),
            ],
            compiler_params=params,
            cost_estimate=pl.CostEstimate(flops=flops, bytes_accessed=8 << 20, transcendentals=0),
            name="last_stage" if last else "stage",
        )(index, send, weights, coef, *fields, own, *edges)

    second, own, west2, east2, row2 = stage(
        0.5 * STEP_SIZE, [state, state], own, halo(west, east, row)
    )
    third, own, west3, east3, row3 = stage(
        0.5 * STEP_SIZE, [state, second], own, halo(west2, east2, row2)
    )
    fourth, own, west4, east4, row4 = stage(
        STEP_SIZE, [state, third], own, halo(west3, east3, row3)
    )
    next_state, final = stage(
        STEP_SIZE / 6.0, [state, second, third, fourth], own, halo(west4, east4, row4), last=True
    )

    ocean_dev, intersections = ovl_local.shape
    turned_interp = pl.pallas_call(
        turn_kernel,
        out_shape=jax.ShapeDtypeStruct((ocean_dev, nodes, intersections * nodes), BF16),
        in_specs=[VMEM],
        out_specs=VMEM,
        compiler_params=params,
        name="turn_interp",
    )(interp)

    final = final.reshape(rows * cols, nodes, feats)
    half = lon_count // 2
    opposite = [(i, (i + half) % lon_count) for i in range(lon_count)]
    seam = (half - 1, lon_count - 1)
    ends = [(0, half - 1), (half - 1, 0), (half, lon_count - 1), (lon_count - 1, half)]
    up = [pair for pair in forward if pair[0] not in seam]
    down = [pair for pair in backward if pair[1] not in seam]
    native = lax.ppermute(final, "lon", ends)
    center = lax.ppermute(final, "lon", opposite)
    below = lax.ppermute(center, "lon", up)
    above = lax.ppermute(center, "lon", down)
    sources = []
    for piece in (below, center, above):
        sources += [piece, lax.ppermute(piece, "lat", swap)]
    other_native = lax.ppermute(native, "lat", swap)

    middle = (my_lon + half) % lon_count
    owners = ovl_owner.reshape(ocean_dev, intersections)
    relative = (owners // lat_count - middle + 1 + lon_count) % lon_count
    away = (owners % lat_count != my_lat).astype(jnp.int32)
    slot = (relative * 2 + away) * (rows * cols) + ovl_local
    in_half = my_lon % half
    ends_at = jnp.stack([in_half == 0, in_half == half - 1]).astype(jnp.int32)
    block = 8
    ocean = pl.pallas_call(
        ocean_kernel,
        grid=(ocean_dev // block,),
        out_shape=jax.ShapeDtypeStruct((ocean_dev, nodes, feats), BF16),
        in_specs=[SMEM, SMEM, pl.BlockSpec((block, nodes, intersections * nodes), lambda g: (g, 0, 0))]
        + [ANY] * 8,
        out_specs=pl.BlockSpec((block, nodes, feats), lambda g: (g, 0, 0)),
        scratch_shapes=[
            pltpu.VMEM((6, rows * cols, nodes, feats), BF16),
            pltpu.SemaphoreType.DMA((6,)),
        ],
        compiler_params=params,
        name="ocean",
    )(slot, ends_at, turned_interp, *sources, native, other_native)
    return next_state, ocean


def solution(mesh):
    placed = (
        P(("member", "lat"), "lon", None, None),
        P(None, "lat", "lon", None, None, None),
        P(None, "lat", "lon", None),
        P("lat", "lon", None),
        P(("lon", "lat"), None, None),
        P(("lon", "lat"), None),
        P(("lon", "lat"), None, None, None),
    )
    return jax.shard_map(
        local,
        mesh=mesh,
        in_specs=placed,
        out_specs=(
            P(("member", "lat"), "lon", None, None),
            P(("member", "lon", "lat"), None, None),
        ),
        check_vma=False,
    )
```

```python
import functools

import jax
import jax.numpy as jnp
from jax import lax
from jax.experimental import pallas as pl
from jax.experimental.pallas import tpu as pltpu
from jax.sharding import PartitionSpec as P

CORIOLIS = 2.0
STEP_SIZE = 0.2
BF16 = jnp.bfloat16
F32 = jnp.float32
VMEM = pl.BlockSpec(memory_space=pltpu.VMEM)
SMEM = pl.BlockSpec(memory_space=pltpu.SMEM)
MIB = 1024 * 1024


def in_vmem(value):
    return pltpu.with_memory_space_constraint(value, pltpu.VMEM)


def vmem_call(kernel, name, outs, scalars, arrays, scratch=(), limit=8, flops=0):
    return pl.pallas_call(
        kernel,
        out_shape=[pltpu.VMEM(shape, dtype) for shape, dtype in outs],
        in_specs=[SMEM] * len(scalars) + [VMEM] * len(arrays),
        out_specs=[VMEM] * len(outs),
        scratch_shapes=list(scratch),
        compiler_params=pltpu.CompilerParams(vmem_limit_bytes=limit * MIB),
        cost_estimate=pl.CostEstimate(flops=flops, bytes_accessed=1 * MIB, transcendentals=0),
        name=name,
    )(*scalars, *[in_vmem(array) for array in arrays])


def prep_kernel(scalar_ref, state_ref, inner_ref, west_ref, east_ref, erow_ref, irow_ref):
    rows, cols = state_ref.shape[:2]
    for a in range(rows):
        west_ref[a, 0] = state_ref[a, 0].astype(BF16)
        east_ref[a, 0] = state_ref[a, cols - 1].astype(BF16)
        for b in range(1, cols - 1):
            inner_ref[a, b - 1] = state_ref[a, b].astype(BF16)
    send = scalar_ref[0]
    erow_ref[0, 0] = west_ref[send, 0]
    erow_ref[0, 1] = east_ref[send, 0]
    irow_ref[0] = inner_ref[send]


def coef_kernel(pos_ref, coef_ref):
    rows, cols, nodes = pos_ref.shape[1:]
    low = lax.broadcasted_iota(jnp.int32, (nodes, nodes), 1) < nodes // 2
    for a in range(rows):
        for b in range(cols):
            x0, x1, x2 = (
                jnp.broadcast_to(pos_ref[c, a, b][None, :], (nodes, nodes)).T for c in range(3)
            )
            spin = CORIOLIS * x2
            coef_ref[a, b, 0] = jnp.where(low, x0, x1)
            coef_ref[a, b, 1] = jnp.where(low, x2, 0.0)
            coef_ref[a, b, 2] = spin * jnp.where(low, x1, -x0)
            coef_ref[a, b, 3] = spin * jnp.where(low, -x2, x2)
            coef_ref[a, b, 4] = jnp.where(low, spin * x0, 0.0)
            coef_ref[a, b, 5] = jnp.where(low, spin * x1, 0.0)


def turned(value):
    return pltpu.roll(value, value.shape[-1] // 2, axis=1)


def tendency(tile, grads, coef, low):
    half = tile.shape[-1] // 2
    sa, sb = tile[:, :half], tile[:, half:]
    ra, rb = turned(sa), turned(sb)
    v0 = jnp.where(low, sa, ra)
    v1 = jnp.where(low, ra, sa)
    v2 = jnp.where(low, sb, rb)
    ga = [g[:, :half] for g in grads]
    gb = [g[:, half:] for g in grads]
    t0a, t0b, t2b = turned(ga[0]), turned(gb[0]), turned(gb[2])
    fa = (
        ga[3]
        - (v0 * ga[0] + v1 * ga[1] + v2 * ga[2])
        - (coef[2] * v2 + coef[3] * ra)
        - jnp.where(low, t0b, gb[1])
    )
    spread = sb * (t0a + ga[1] + t2b)
    fb = (
        gb[3]
        - (v0 * gb[0] + v1 * gb[1] + v2 * gb[2])
        - (coef[4] * v1 - coef[5] * v0)
        - jnp.where(low, t2b, spread)
    )
    part = coef[0] * fa + coef[1] * fb
    radial = part + turned(part)
    return fa - coef[0] * radial, fb - coef[1] * radial


def stage_kernel(edge, first, last, scale, scalar_ref, w_ref, coef_ref, state_ref, *refs):
    refs = list(refs)
    ext = refs.pop()
    rows, cols, nodes, feats = state_ref.shape
    taps = w_ref.shape[3]
    columns = (0, cols - 1) if edge else tuple(range(1, cols - 1))

    def take(count):
        taken, refs[:count] = refs[:count], []
        return taken

    older = take(2) if last else []
    now_ref = None if first else take(1)[0]
    inner_ref, west_ref, east_ref, erow_ref, irow_ref = take(5)
    for a in range(rows):
        ext[a, 1] = west_ref[a, 0]
        ext[a, cols] = east_ref[a, 0]
        for b in range(cols - 2):
            ext[a, b + 2] = inner_ref[a, b]
    ext[rows, 1] = erow_ref[0, 0]
    ext[rows, cols] = erow_ref[0, 1]
    for b in range(cols - 2):
        ext[rows, b + 2] = irow_ref[0, b]
    send = scalar_ref[0]
    if edge:
        fwest_ref, feast_ref, cwest_ref, ceast_ref = take(4)
        for a in range(rows):
            ext[a, 0] = fwest_ref[a, 0]
            ext[a, cols + 1] = feast_ref[a, 0]
        ext[rows, 0] = cwest_ref[1 - send, 0]
        ext[rows, cols + 1] = ceast_ref[1 - send, 0]

    next_ref, *outs = refs
    low = lax.broadcasted_iota(jnp.int32, (nodes, feats // 2), 1) < feats // 4
    for a in range(rows):
        for place, b in enumerate(columns):
            base = 1 + (a * cols + b) * taps
            where = [scalar_ref[base + k] for k in range(taps)]
            near = jnp.concatenate([ext[w // (cols + 2), w % (cols + 2)] for w in where], axis=0)
            weights = jnp.concatenate(
                [
                    jnp.concatenate([w_ref[q, a, b, k] for k in range(taps)], axis=1)
                    for q in range(4)
                ],
                axis=0,
            )
            derivs = jnp.dot(weights, near, preferred_element_type=F32)
            grads = [derivs[q * nodes : (q + 1) * nodes] for q in range(4)]
            coef = [coef_ref[a, b, i] for i in range(6)]
            now = state_ref[a, b] if first else now_ref[a, place]
            rate = jnp.concatenate(tendency(now, grads, coef, low), axis=1)
            if last:
                out = (1.0 / 3.0) * (
                    older[0][a, place] + 2.0 * older[1][a, place] + now - state_ref[a, b]
                ) + scale * rate
            else:
                out = state_ref[a, b] + scale * rate
            next_ref[a, place] = out
            rounded = out.astype(BF16)
            if last or not edge:
                outs[0][a, place] = rounded
            else:
                outs[place][a, 0] = rounded
    if not last:
        if edge:
            outs[2][0, 0] = outs[0][send, 0]
            outs[2][0, 1] = outs[1][send, 0]
        else:
            outs[1][0] = outs[0][send]


def turn_kernel(interp_ref, out_ref):
    tiles, taps, nodes, points = interp_ref.shape
    for o in range(tiles):
        out_ref[o] = interp_ref[o].reshape(taps * nodes, points).T


def ocean_kernel(chunks, scalar_ref, interp_ref, *refs):
    *sources, out_ref, tiles = refs
    size = sources[0].shape[0] * sources[0].shape[1]
    flat = [source.reshape(size, *source.shape[2:]) for source in sources]
    per = 2 * chunks

    @pl.when(pl.program_id(0) == 0)
    def _():
        for side, flag in ((0, scalar_ref[0]), (1, None), (2, scalar_ref[1])):
            for part in range(per):
                place = (side * per + part) * size
                if flag is None:
                    tiles[pl.ds(place, size)] = flat[side * per + part][...]
                else:

                    @pl.when(flag == 0)
                    def _():
                        tiles[pl.ds(place, size)] = flat[side * per + part][...]

                    @pl.when(flag == 1)
                    def _():
                        tiles[pl.ds(place, size)] = flat[3 * per + part][...]

    block = interp_ref.shape[0]
    taps = 2
    base = 2 + pl.program_id(0) * (block * taps)
    for o in range(block):
        near = jnp.concatenate(
            [tiles[scalar_ref[base + o * taps + j]] for j in range(taps)], axis=0
        )
        out_ref[o] = jnp.dot(interp_ref[o], near, preferred_element_type=F32).astype(BF16)


def local(state, weights, positions, stencil_codes, ovl_owner, ovl_local, interp):
    rows, cols, nodes, feats = state.shape
    taps = stencil_codes.shape[-1]
    lon_count = lax.axis_size("lon")
    lat_count = lax.axis_size("lat")
    my_lon = lax.axis_index("lon")
    my_lat = lax.axis_index("lat")
    forward = [(i, (i + 1) % lon_count) for i in range(lon_count)]
    backward = [(target, source) for source, target in forward]
    swap = [(i, lat_count - 1 - i) for i in range(lat_count)]

    tile_row = lax.broadcasted_iota(jnp.int32, stencil_codes.shape, 0)
    tile_col = lax.broadcasted_iota(jnp.int32, stencil_codes.shape, 1)
    ext_row = tile_row + stencil_codes // 3 - 1
    ext_row = jnp.where(ext_row < 0, rows, ext_row)
    index = ext_row * (cols + 2) + tile_col + stencil_codes % 3
    send = (1 - my_lat).astype(jnp.int32).reshape(1)
    scalars = jnp.concatenate([send, index.reshape(-1)])

    inner_cols = cols - 2
    tile = (nodes, feats)
    west_s = ((rows, 1) + tile, BF16)
    inner_s = ((rows, inner_cols) + tile, BF16)
    erow_s = ((1, 2) + tile, BF16)
    irow_s = ((1, inner_cols) + tile, BF16)

    inner, west, east, erow, irow = vmem_call(
        prep_kernel, "prep", [inner_s, west_s, west_s, erow_s, irow_s], [send], [state]
    )
    (coef,) = vmem_call(
        coef_kernel, "coef", [((rows, cols, 6, nodes, nodes), F32)], [], [positions]
    )

    def flip(value):
        return lax.ppermute(value, "lat", swap)

    flops = 2 * 4 * rows * taps * nodes * nodes * feats

    def stage(scale, fields_i, fields_e, own, first=False, last=False):
        inner, west, east, erow, irow = own
        from_west = lax.ppermute(east, "lon", forward)
        from_east = lax.ppermute(west, "lon", backward)
        near = [inner, west, east, flip(erow), flip(irow)]
        far = [from_west, from_east, flip(from_west), flip(from_east)]
        results = []
        for edge in (False, True):
            width = 2 if edge else inner_cols
            outs = [((rows, width) + tile, F32)]
            if last:
                outs += [((rows, width) + tile, BF16)]
            else:
                outs += [west_s, west_s, erow_s] if edge else [inner_s, irow_s]
            results.append(
                vmem_call(
                    functools.partial(stage_kernel, edge, first, last, scale),
                    ("edge" if edge else "inner") + ("_last" if last else ""),
                    outs,
                    [scalars],
                    [weights, coef, state]
                    + (fields_e if edge else fields_i)
                    + near
                    + (far if edge else []),
                    [pltpu.VMEM((rows + 1, cols + 2) + tile, BF16)],
                    flops=flops * width,
                )
            )
        return results

    own = (inner, west, east, erow, irow)
    half_step = 0.5 * STEP_SIZE
    (i2, inner, irow), (e2, west, east, erow) = stage(half_step, [], [], own, first=True)
    own = (inner, west, east, erow, irow)
    (i3, inner, irow), (e3, west, east, erow) = stage(half_step, [i2], [e2], own)
    own = (inner, west, east, erow, irow)
    (i4, inner, irow), (e4, west, east, erow) = stage(STEP_SIZE, [i3], [e3], own)
    own = (inner, west, east, erow, irow)
    (next_i, final_i), (next_e, final_e) = stage(
        STEP_SIZE / 6.0, [i2, i3, i4], [e2, e3, e4], own, last=True
    )
    next_state = jnp.concatenate([next_e[:, :1], next_i, next_e[:, 1:]], axis=1)

    ocean_dev, intersections = ovl_local.shape
    (turned_interp,) = vmem_call(
        turn_kernel,
        "turn_interp",
        [((ocean_dev, nodes, intersections * nodes), BF16)],
        [],
        [interp],
    )

    half = lon_count // 2
    opposite = [(i, (i + half) % lon_count) for i in range(lon_count)]
    seam = (half - 1, lon_count - 1)
    ends = [(0, half - 1), (half - 1, 0), (half, lon_count - 1), (lon_count - 1, half)]
    up = [pair for pair in forward if pair[0] not in seam]
    down = [pair for pair in backward if pair[1] not in seam]
    below, center, above, native = [], [], [], []
    chunks = [final_i, final_e]
    for final in chunks:
        native.append(lax.ppermute(final, "lon", ends))
        center.append(lax.ppermute(final, "lon", opposite))
        below.append(lax.ppermute(center[-1], "lon", up))
        above.append(lax.ppermute(center[-1], "lon", down))
    sources = []
    for pieces in (below, center, above, native):
        sources += pieces + [flip(piece) for piece in pieces]

    middle = (my_lon + half) % lon_count
    owners = ovl_owner.reshape(ocean_dev, intersections)
    relative = (owners // lat_count - middle + 1 + lon_count) % lon_count
    away = (owners % lat_count != my_lat).astype(jnp.int32)
    tile_row, tile_col = ovl_local // cols, ovl_local % cols
    is_edge = (tile_col == 0) | (tile_col == cols - 1)
    chunk = is_edge.astype(jnp.int32)
    within = jnp.where(
        is_edge, tile_row * 2 + (tile_col == cols - 1), tile_row * inner_cols + tile_col - 1
    )
    per_chunk = rows * inner_cols
    slot = ((relative * 2 + away) * 2 + chunk) * per_chunk + within
    in_half = my_lon % half
    at_ends = jnp.stack([in_half == 0, in_half == half - 1]).astype(jnp.int32)
    ocean_scalars = jnp.concatenate([at_ends, slot.reshape(-1).astype(jnp.int32)])
    block = 8
    ocean = pl.pallas_call(
        functools.partial(ocean_kernel, len(chunks)),
        grid=(ocean_dev // block,),
        out_shape=jax.ShapeDtypeStruct((ocean_dev, nodes, feats), BF16),
        in_specs=[SMEM, pl.BlockSpec((block, nodes, intersections * nodes), lambda g: (g, 0, 0))]
        + [VMEM] * len(sources),
        out_specs=pl.BlockSpec((block, nodes, feats), lambda g: (g, 0, 0)),
        scratch_shapes=[pltpu.VMEM((6 * rows * cols, nodes, feats), BF16)],
        compiler_params=pltpu.CompilerParams(vmem_limit_bytes=16 * MIB),
        name="ocean",
    )(ocean_scalars, turned_interp, *[in_vmem(source) for source in sources])
    return next_state, ocean


def solution(mesh):
    placed = (
        P(("member", "lat"), "lon", None, None),
        P(None, "lat", "lon", None, None, None),
        P(None, "lat", "lon", None),
        P("lat", "lon", None),
        P(("lon", "lat"), None, None),
        P(("lon", "lat"), None),
        P(("lon", "lat"), None, None, None),
    )
    return jax.shard_map(
        local,
        mesh=mesh,
        in_specs=placed,
        out_specs=(
            P(("member", "lat"), "lon", None, None),
            P(("member", "lon", "lat"), None, None),
        ),
        check_vma=False,
    )
```

```python
import functools

import jax
import jax.numpy as jnp
from jax import lax
from jax.experimental import pallas as pl
from jax.experimental.pallas import tpu as pltpu
from jax.sharding import PartitionSpec as P

CORIOLIS = 2.0
STEP_SIZE = 0.2
BF16 = jnp.bfloat16
F32 = jnp.float32
VMEM = pl.BlockSpec(memory_space=pltpu.VMEM)
HBM = pl.BlockSpec(memory_space=pltpu.HBM)
MIB = 1024 * 1024


def in_vmem(value):
    return pltpu.with_memory_space_constraint(value, pltpu.VMEM)


def in_hbm(value):
    return pltpu.with_memory_space_constraint(value, pltpu.HBM)


def vmem_call(kernel, name, outs, arrays, scratch=(), limit=4, aliases=None):
    return pl.pallas_call(
        kernel,
        out_shape=[pltpu.VMEM(shape, dtype) for shape, dtype in outs],
        in_specs=[VMEM] * len(arrays),
        out_specs=[VMEM] * len(outs),
        scratch_shapes=list(scratch),
        compiler_params=pltpu.CompilerParams(vmem_limit_bytes=limit * MIB),
        cost_estimate=pl.CostEstimate(flops=1000, bytes_accessed=1000, transcendentals=0),
        input_output_aliases=aliases or {},
        name=name,
    )(*[in_vmem(array) for array in arrays])


def after(value, *others):
    return lax.optimization_barrier((value,) + others)[0]


def prep_kernel(scalar_ref, state_ref, inner_ref, irow_ref, edge_a_ref, edge_b_ref, erow_ref):
    rows, cols = state_ref.shape[:2]
    for a in range(rows):
        edge_a_ref[a, 0] = state_ref[a, scalar_ref[0, 1]].astype(BF16)
        edge_b_ref[a, 0] = state_ref[a, scalar_ref[0, cols]].astype(BF16)
        for c in range(1, cols - 1):
            inner_ref[a, c - 1] = state_ref[a, scalar_ref[0, 1 + c]].astype(BF16)
    send = scalar_ref[0, 0]
    irow_ref[0] = inner_ref[send]
    erow_ref[0, 0] = edge_a_ref[send, 0]
    erow_ref[0, 1] = edge_b_ref[send, 0]


def setup_kernel(scalar_ref, pos_ref, w_ref, coef_ref, inner_ref, edge_ref, sems):
    copies = []
    for c in range(pos_ref.shape[2]):
        on_edge = c in (0, pos_ref.shape[2] - 1)
        target, place = (edge_ref, min(c, 1)) if on_edge else (inner_ref, c - 1)
        copies.append(
            pltpu.make_async_copy(
                w_ref.at[:, :, pl.ds(scalar_ref[0, 1 + c], 1)],
                target.at[:, :, pl.ds(place, 1)],
                sems.at[c],
            )
        )
    for copy in copies:
        copy.start()
    rows, cols, nodes = pos_ref.shape[1:]
    low = lax.broadcasted_iota(jnp.int32, (nodes, nodes), 1) < nodes // 2
    for a in range(rows):
        for b in range(cols):
            x0, x1, x2 = (
                jnp.broadcast_to(pos_ref[c, a, b][None, :], (nodes, nodes)).T for c in range(3)
            )
            coef_ref[a, b, 0] = jnp.where(low, x0, x1)
            coef_ref[a, b, 1] = x2
    for copy in copies:
        copy.wait()


def turn_kernel(interp_ref, turned_ref, interp, sem):
    copy = pltpu.make_async_copy(interp_ref, interp, sem)
    copy.start()
    copy.wait()
    tiles, taps, nodes, points = interp.shape
    for o in range(tiles):
        turned_ref[o] = interp[o].reshape(taps * nodes, points).T


def turned(value):
    return pltpu.roll(value, value.shape[-1] // 2, axis=1)


def tendency(tile, grads, x01, x2, low):
    half = tile.shape[-1] // 2
    sa, sb = tile[:, :half], tile[:, half:]
    ra, rb = turned(sa), turned(sb)
    v0 = jnp.where(low, sa, ra)
    v1 = jnp.where(low, ra, sa)
    v2 = jnp.where(low, sb, rb)
    ga = [g[:, :half] for g in grads]
    gb = [g[:, half:] for g in grads]
    t0a, t0b, t2b = turned(ga[0]), turned(gb[0]), turned(gb[2])
    x10 = turned(x01)
    spin = CORIOLIS * x2
    cross = spin * (x10 * v2 - x2 * ra)
    fa = (
        ga[3]
        - (v0 * ga[0] + v1 * ga[1] + v2 * ga[2])
        - jnp.where(low, cross + t0b, gb[1] - cross)
    )
    spread = sb * (t0a + ga[1] + t2b)
    fb = (
        gb[3]
        - (v0 * gb[0] + v1 * gb[1] + v2 * gb[2])
        - jnp.where(low, spin * (x01 * v1 - x10 * v0) + t2b, spread)
    )
    x2_low = jnp.where(low, x2, 0.0)
    part = x01 * fa + x2_low * fb
    radial = part + turned(part)
    return fa - x01 * radial, fb - x2_low * radial


def stage_kernel(edge, number, stages, scale, scalar_ref, w_ref, coef_ref, *refs):
    refs = list(refs)
    ext = refs.pop()
    rows, cols = coef_ref.shape[:2]
    nodes, feats = ext.shape[1:]
    taps = w_ref.shape[3]
    wide = cols + 2
    last = number == stages - 1
    blend = number == stages - 2
    state_ref = None if last else refs.pop(0)
    sum_ref = refs.pop(0) if last or blend else None
    now_ref = refs.pop(0) if number else None
    inner_ref, irow_ref, edge_a_ref, edge_b_ref, erow_ref = refs[:5]
    refs = refs[5:]
    send = scalar_ref[0, 0]
    for a in range(rows):
        ext[a * wide + 1] = edge_a_ref[a, 0]
        ext[a * wide + cols] = edge_b_ref[a, 0]
        ext[pl.ds(a * wide + 2, cols - 2)] = inner_ref[a]
    ext[rows * wide + 1] = erow_ref[0, 0]
    ext[rows * wide + cols] = erow_ref[0, 1]
    ext[pl.ds(rows * wide + 2, cols - 2)] = irow_ref[0]
    if edge:
        halo_a_ref, halo_b_ref, corner_a_ref, corner_b_ref = refs[:4]
        refs = refs[4:]
        for a in range(rows):
            ext[a * wide] = halo_a_ref[a, 0]
            ext[a * wide + cols + 1] = halo_b_ref[a, 0]
        ext[rows * wide] = corner_a_ref[1 - send, 0]
        ext[rows * wide + cols + 1] = corner_b_ref[1 - send, 0]
    blend_ref = refs.pop(0) if blend else None
    next_ref, *outs = refs
    columns = (0, cols - 1) if edge else tuple(range(1, cols - 1))
    low = lax.broadcasted_iota(jnp.int32, (nodes, feats // 2), 1) < feats // 4
    for a in range(rows):
        for place, c in enumerate(columns):
            b = scalar_ref[0, 1 + c]
            base = 1 + cols + (a * cols + c) * taps
            near = jnp.concatenate([ext[scalar_ref[0, base + k]] for k in range(taps)], axis=0)
            weights = jnp.concatenate(
                [
                    jnp.concatenate([w_ref[q, a, place, k] for k in range(taps)], axis=1)
                    for q in range(4)
                ],
                axis=0,
            )
            derivs = jnp.dot(weights, near, preferred_element_type=F32)
            grads = [derivs[q * nodes : (q + 1) * nodes] for q in range(4)]
            now = now_ref[a, place] if number else state_ref[a, b]
            x01, x2 = coef_ref[a, b, 0], coef_ref[a, b, 1]
            rate = jnp.concatenate(tendency(now, grads, x01, x2, low), axis=1)
            out = (sum_ref[a, place] if last else state_ref[a, b]) + scale * rate
            if blend:
                blend_ref[a, place] = (1.0 / 3.0) * (
                    sum_ref[a, place] + 2.0 * now + out - state_ref[a, b]
                )
            next_ref[a, place] = out
            rounded = out.astype(BF16)
            if edge and not last:
                outs[place][a, 0] = rounded
            else:
                outs[0][a, place] = rounded
    if not last:
        if edge:
            outs[2][0, 0] = outs[0][send, 0]
            outs[2][0, 1] = outs[1][send, 0]
        else:
            outs[1][0] = outs[0][send]


def join_kernel(scalar_ref, inner_ref, edge_ref, out_ref):
    rows, cols = out_ref.shape[:2]
    for a in range(rows):
        for c in range(cols):
            source = edge_ref[a, c // (cols - 1)] if c in (0, cols - 1) else inner_ref[a, c - 1]
            out_ref[a, scalar_ref[0, 1 + c]] = source


def pick_kernel(flag, scalar_ref, first_ref, *refs):
    count = len(refs) // 2
    for i in range(count):
        refs[count + i][...] = jnp.where(
            scalar_ref[0, flag + i] == 1, first_ref[...], refs[i][...]
        )


def collect_kernel(places, *refs):
    pieces, out_ref = refs[-1 - len(places) : -1], refs[-1]
    for place, piece in zip(places, pieces):
        flat = piece.reshape(piece.shape[0] * piece.shape[1], *piece.shape[2:])
        out_ref[pl.ds(place, flat.shape[0])] = flat[...]


def ocean_kernel(scalar_ref, interp_ref, tiles_ref, out_ref):
    block = out_ref.shape[0]
    taps = scalar_ref.shape[1]
    first = pl.program_id(0) * block
    for o in range(block):
        near = jnp.concatenate(
            [tiles_ref[scalar_ref[first + o, j]] for j in range(taps)], axis=0
        )
        out_ref[o] = jnp.dot(interp_ref[first + o], near, preferred_element_type=F32).astype(BF16)


def local(state, weights, positions, stencil_codes, ovl_owner, ovl_local, interp):
    rows, cols, nodes, feats = state.shape
    taps = stencil_codes.shape[-1]
    lon_count = lax.axis_size("lon")
    lat_count = lax.axis_size("lat")
    my_lon = lax.axis_index("lon")
    my_lat = lax.axis_index("lat")
    to_a = [(i, i ^ 1) for i in range(lon_count)]
    to_b = [(i, (i + 1 if i % 2 else i - 1) % lon_count) for i in range(lon_count)]
    swap = [(i, lat_count - 1 - i) for i in range(lat_count)]

    def flip(value):
        return lax.ppermute(value, "lat", swap)

    a_is_east = my_lon % 2 == 0
    tile_row = lax.broadcasted_iota(jnp.int32, stencil_codes.shape, 0)
    tile_col = lax.broadcasted_iota(jnp.int32, stencil_codes.shape, 1)
    near_col = tile_col + stencil_codes % 3 - 1
    ext_row = tile_row + stencil_codes // 3 - 1
    ext_row = jnp.where(ext_row < 0, rows, ext_row)
    ext_col = jnp.where(a_is_east, cols - 1 - near_col, near_col)
    index = ext_row * (cols + 2) + ext_col + 1
    index = jnp.where(a_is_east, index[:, ::-1], index)
    order = jnp.arange(cols, dtype=jnp.int32)
    order = jnp.where(a_is_east, cols - 1 - order, order)
    send = (1 - my_lat).astype(jnp.int32).reshape(1)

    def as_row(parts):
        flat = jnp.concatenate([part.reshape(-1).astype(jnp.int32) for part in parts])
        return jnp.pad(flat, (0, -flat.size % 128)).reshape(1, -1)

    middle = lon_count // 2
    in_half = my_lon % middle
    ocean_dev, intersections = ovl_local.shape
    target = (my_lon + middle) % lon_count
    owners = ovl_owner.reshape(ocean_dev, intersections)
    owner_lon = owners // lat_count
    relative = (owner_lon - target + 1 + lon_count) % lon_count
    kind = jnp.where(relative == 1, 0, jnp.where((relative == 2) == a_is_east, 1, 2))
    away = (owners % lat_count != my_lat).astype(jnp.int32)
    owner_row, owner_col = ovl_local // cols, ovl_local % cols
    owner_col = jnp.where(owner_lon % 2 == 0, cols - 1 - owner_col, owner_col)
    inner_count = rows * (cols - 2)
    inner_slot = (kind * 2 + away) * inner_count + owner_row * (cols - 2) + owner_col - 1
    edge_slot = 6 * inner_count + (relative * 2 + away) * (2 * rows)
    edge_slot += 2 * owner_row + (owner_col != 0)
    slot = jnp.where((owner_col == 0) | (owner_col == cols - 1), edge_slot, inner_slot)

    turns = (in_half == middle - 2) | (in_half == 1)
    scalars = as_row([send, order, index, turns, in_half == middle - 1, in_half == 0])
    flags = 1 + cols + index.size

    tile = (nodes, feats)
    inner_s = ((rows, cols - 2) + tile, BF16)
    irow_s = ((1, cols - 2) + tile, BF16)
    edge_s = ((rows, 1) + tile, BF16)
    erow_s = ((1, 2) + tile, BF16)

    own = vmem_call(
        prep_kernel,
        "prep",
        [inner_s, irow_s, edge_s, edge_s, erow_s],
        [as_row([send, order]), state],
    )

    quarter = weights.shape[:2]
    coef, w_inner, w_edge = pl.pallas_call(
        setup_kernel,
        out_shape=[
            pltpu.VMEM((rows, cols, 2, nodes, nodes), F32),
            pltpu.VMEM(quarter + (cols - 2,) + weights.shape[3:], BF16),
            pltpu.VMEM(quarter + (2,) + weights.shape[3:], BF16),
        ],
        in_specs=[VMEM, VMEM, HBM],
        out_specs=[VMEM] * 3,
        scratch_shapes=[pltpu.SemaphoreType.DMA((cols,))],
        compiler_params=pltpu.CompilerParams(vmem_limit_bytes=4 * MIB),
        name="setup",
    )(in_vmem(scalars), in_vmem(after(positions, slot)), in_hbm(weights))
    scales = (0.5 * STEP_SIZE, 0.5 * STEP_SIZE, STEP_SIZE, STEP_SIZE / 6.0)
    stages = len(scales)

    fields = {False: [], True: []}
    for number, scale in enumerate(scales):
        last = number == stages - 1
        blend = number == stages - 2
        inner, irow, edge_a, edge_b, erow = own
        halo_a = lax.ppermute(edge_a, "lon", to_a)
        halo_b = lax.ppermute(edge_b, "lon", to_b)
        if number == 0:
            halo_a = after(halo_a, w_edge)
        near = [inner, flip(irow), edge_a, edge_b, flip(erow)]
        far = [halo_a, halo_b, flip(halo_a), flip(halo_b)]
        own = []
        for edge in (False, True):
            field_s = ((rows, 2 if edge else cols - 2) + tile, F32)
            outs = [edge_s, edge_s, erow_s] if edge else [inner_s, irow_s]
            if last:
                outs = [((rows, 2 if edge else cols - 2) + tile, BF16)]
            outs = ([field_s] if blend else []) + [field_s] + outs
            results = vmem_call(
                functools.partial(stage_kernel, edge, number, stages, scale),
                ("edge" if edge else "inner") + ("_last" if last else ""),
                outs,
                [scalars, w_edge if edge else w_inner, coef]
                + ([] if last else [state])
                + fields[edge]
                + near
                + (far if edge else []),
                [pltpu.VMEM(((rows + 1) * (cols + 2),) + tile, BF16)],
            )
            if blend:
                fields[edge], results = list(results[:2]), results[2:]
            else:
                fields[edge], results = (fields[edge] + [results[0]])[-2:], results[1:]
            own += results
    next_i, next_e = fields[False][-1], fields[True][-1]
    final_i, final_e = own

    (next_state,) = pl.pallas_call(
        join_kernel,
        out_shape=[jax.ShapeDtypeStruct(state.shape, F32)],
        in_specs=[VMEM] * 3,
        out_specs=[VMEM],
        compiler_params=pltpu.CompilerParams(vmem_limit_bytes=4 * MIB),
        name="join",
    )(scalars, next_i, next_e)
    turned_interp = pl.pallas_call(
        turn_kernel,
        out_shape=pltpu.VMEM((ocean_dev, nodes, intersections * nodes), BF16),
        in_specs=[HBM],
        out_specs=VMEM,
        scratch_shapes=[pltpu.VMEM(interp.shape, BF16), pltpu.SemaphoreType.DMA(())],
        compiler_params=pltpu.CompilerParams(vmem_limit_bytes=4 * MIB),
        name="turn_interp",
    )(in_hbm(after(interp, next_e)))

    opposite = [(i, (i + middle) % lon_count) for i in range(lon_count)]

    def within_half(step):
        return [(i, i - i % middle + (i + step(i)) % middle) for i in range(lon_count)]

    up, down = within_half(lambda i: 1), within_half(lambda i: -1)
    onward = within_half(lambda i: -2 if i % 2 else 2)

    def pick(flag, *pieces):
        return vmem_call(
            functools.partial(pick_kernel, flag),
            "pick",
            [(pieces[0].shape, BF16)] * (len(pieces) - 1),
            [scalars, *pieces],
        )

    def collect(tiles, place, pieces):
        size = pieces[0].shape[0] * pieces[0].shape[1]
        return vmem_call(
            functools.partial(collect_kernel, [place + i * size for i in range(len(pieces))]),
            "collect",
            [((6 * rows * cols,) + tile, BF16)],
            ([] if tiles is None else [tiles]) + pieces,
            aliases=None if tiles is None else {0: 0},
        )[0]

    final_i = after(final_i, halo_a, halo_b)
    center_i = lax.ppermute(final_i, "lon", opposite)
    native = lax.ppermute(final_i, "lon", to_a)
    center_e = lax.ppermute(after(final_e, center_i, next_state, turned_interp), "lon", opposite)
    paired = lax.ppermute(after(center_i, native, next_state, turned_interp), "lon", to_a)
    passed = lax.ppermute(pick(flags, native, paired)[0], "lon", onward)
    tiles = collect(
        None, 0, [center_i, flip(center_i), paired, flip(paired), passed, flip(passed)]
    )
    going_up, going_down = pick(flags + 1, final_e, center_e, center_e)
    below = lax.ppermute(going_up, "lon", up)
    above = lax.ppermute(going_down, "lon", down)
    tiles = collect(
        tiles,
        6 * inner_count,
        [below, flip(below), center_e, flip(center_e), above, flip(above)],
    )
    block = 8
    ocean = pl.pallas_call(
        ocean_kernel,
        grid=(ocean_dev // block,),
        out_shape=jax.ShapeDtypeStruct((ocean_dev, nodes, feats), BF16),
        in_specs=[VMEM] * 3,
        out_specs=pl.BlockSpec((block, nodes, feats), lambda g: (g, 0, 0)),
        compiler_params=pltpu.CompilerParams(vmem_limit_bytes=4 * MIB),
        name="ocean",
    )(in_vmem(slot), in_vmem(turned_interp), in_vmem(tiles))
    return next_state, ocean


def solution(mesh):
    placed = (
        P(("member", "lat"), "lon", None, None),
        P(None, "lat", "lon", None, None, None),
        P(None, "lat", "lon", None),
        P("lat", "lon", None),
        P(("lon", "lat"), None, None),
        P(("lon", "lat"), None),
        P(("lon", "lat"), None, None, None),
    )
    return jax.shard_map(
        local,
        mesh=mesh,
        in_specs=placed,
        out_specs=(
            P(("member", "lat"), "lon", None, None),
            P(("member", "lon", "lat"), None, None),
        ),
        check_vma=False,
    )
```

```python
import functools

import jax
import jax.numpy as jnp
from jax import lax
from jax.experimental import pallas as pl
from jax.experimental.pallas import tpu as pltpu
from jax.sharding import PartitionSpec as P

CORIOLIS = 2.0
STEP_SIZE = 0.2
BF16 = jnp.bfloat16
F32 = jnp.float32
VMEM = pl.BlockSpec(memory_space=pltpu.VMEM)
HBM = pl.BlockSpec(memory_space=pltpu.HBM)
MIB = 1024 * 1024


def in_vmem(value):
    return pltpu.with_memory_space_constraint(value, pltpu.VMEM)


def in_hbm(value):
    return pltpu.with_memory_space_constraint(value, pltpu.HBM)


def vmem_call(kernel, name, outs, arrays, scratch=(), limit=4, aliases=None):
    return pl.pallas_call(
        kernel,
        out_shape=[pltpu.VMEM(shape, dtype) for shape, dtype in outs],
        in_specs=[VMEM] * len(arrays),
        out_specs=[VMEM] * len(outs),
        scratch_shapes=list(scratch),
        compiler_params=pltpu.CompilerParams(vmem_limit_bytes=limit * MIB),
        cost_estimate=pl.CostEstimate(flops=1000, bytes_accessed=1000, transcendentals=0),
        input_output_aliases=aliases or {},
        name=name,
    )(*[in_vmem(array) for array in arrays])


def after(value, *others):
    return lax.optimization_barrier((value,) + others)[0]


def prep_kernel(scalar_ref, state_ref, inner_ref, irow_ref, edge_a_ref, edge_b_ref, erow_ref):
    rows, cols = state_ref.shape[:2]
    for a in range(rows):
        edge_a_ref[a, 0] = state_ref[a, scalar_ref[0, 1]].astype(BF16)
        edge_b_ref[a, 0] = state_ref[a, scalar_ref[0, cols]].astype(BF16)
        for c in range(1, cols - 1):
            inner_ref[a, c - 1] = state_ref[a, scalar_ref[0, 1 + c]].astype(BF16)
    send = scalar_ref[0, 0]
    irow_ref[0] = inner_ref[send]
    erow_ref[0, 0] = edge_a_ref[send, 0]
    erow_ref[0, 1] = edge_b_ref[send, 0]


def setup_kernel(
    scalar_ref, pos_hbm, codes_hbm, w_ref, coef_ref, codes_ref, inner_ref, edge_ref, pos_ref, sems, small_sems
):
    small = [
        pltpu.make_async_copy(pos_hbm, pos_ref, small_sems.at[0]),
        pltpu.make_async_copy(codes_hbm, codes_ref, small_sems.at[1]),
    ]
    for copy in small:
        copy.start()
    rows, cols, nodes = pos_ref.shape[1:]
    copies = []
    for c in range(cols):
        on_edge = c in (0, cols - 1)
        target, place = (edge_ref, min(c, 1)) if on_edge else (inner_ref, c - 1)
        for q in range(w_ref.shape[0]):
            copies.append(
                pltpu.make_async_copy(
                    w_ref.at[q, :, pl.ds(scalar_ref[0, 1 + c], 1)],
                    target.at[q, :, pl.ds(place, 1)],
                    sems.at[q, c],
                )
            )
    for copy in copies:
        copy.start()
    for copy in small:
        copy.wait()
    low = lax.broadcasted_iota(jnp.int32, (nodes, nodes), 1) < nodes // 2
    for a in range(rows):
        for b in range(cols):
            x0, x1, x2 = (
                jnp.broadcast_to(pos_ref[c, a, b][None, :], (nodes, nodes)).T for c in range(3)
            )
            coef_ref[a, b, 0] = jnp.where(low, x0, x1)
            coef_ref[a, b, 1] = x2
    for copy in copies:
        copy.wait()


def turn_kernel(interp_ref, turned_ref, interp, sem):
    copy = pltpu.make_async_copy(interp_ref, interp, sem)
    copy.start()
    copy.wait()
    tiles, taps, nodes, points = interp.shape
    for o in range(tiles):
        turned_ref[o] = interp[o].reshape(taps * nodes, points).T


def turned(value):
    return pltpu.roll(value, value.shape[-1] // 2, axis=1)


def tendency(tile, grads, x01, x2, low):
    half = tile.shape[-1] // 2
    sa, sb = tile[:, :half], tile[:, half:]
    ra, rb = turned(sa), turned(sb)
    v0 = jnp.where(low, sa, ra)
    v1 = jnp.where(low, ra, sa)
    v2 = jnp.where(low, sb, rb)
    ga = [g[:, :half] for g in grads]
    gb = [g[:, half:] for g in grads]
    t0a, t0b, t2b = turned(ga[0]), turned(gb[0]), turned(gb[2])
    x10 = turned(x01)
    spin = CORIOLIS * x2
    cross = spin * (x10 * v2 - x2 * ra)
    fa = (
        ga[3]
        - (v0 * ga[0] + v1 * ga[1] + v2 * ga[2])
        - jnp.where(low, cross + t0b, gb[1] - cross)
    )
    spread = sb * (t0a + ga[1] + t2b)
    fb = (
        gb[3]
        - (v0 * gb[0] + v1 * gb[1] + v2 * gb[2])
        - jnp.where(low, spin * (x01 * v1 - x10 * v0) + t2b, spread)
    )
    x2_low = jnp.where(low, x2, 0.0)
    part = x01 * fa + x2_low * fb
    radial = part + turned(part)
    return fa - x01 * radial, fb - x2_low * radial


def stage_kernel(edge, number, stages, scale, scalar_ref, codes_ref, w_ref, coef_ref, *refs):
    refs = list(refs)
    ext = refs.pop()
    rows, cols = coef_ref.shape[:2]
    nodes, feats = ext.shape[1:]
    taps = w_ref.shape[3]
    wide = cols + 2
    last = number == stages - 1
    blend = number == stages - 2
    state_ref = None if last else refs.pop(0)
    sum_ref = refs.pop(0) if last or blend else None
    now_ref = refs.pop(0) if number else None
    inner_ref, irow_ref, edge_a_ref, edge_b_ref, erow_ref = refs[:5]
    refs = refs[5:]
    send = scalar_ref[0, 0]
    for a in range(rows):
        ext[a * wide + 1] = edge_a_ref[a, 0]
        ext[a * wide + cols] = edge_b_ref[a, 0]
        ext[pl.ds(a * wide + 2, cols - 2)] = inner_ref[a]
    ext[rows * wide + 1] = erow_ref[0, 0]
    ext[rows * wide + cols] = erow_ref[0, 1]
    ext[pl.ds(rows * wide + 2, cols - 2)] = irow_ref[0]
    if edge:
        halo_a_ref, halo_b_ref, corner_a_ref, corner_b_ref = refs[:4]
        refs = refs[4:]
        for a in range(rows):
            ext[a * wide] = halo_a_ref[a, 0]
            ext[a * wide + cols + 1] = halo_b_ref[a, 0]
        ext[rows * wide] = corner_a_ref[1 - send, 0]
        ext[rows * wide + cols + 1] = corner_b_ref[1 - send, 0]
    blend_ref = refs.pop(0) if blend else None
    next_ref, *outs = refs
    columns = (0, cols - 1) if edge else tuple(range(1, cols - 1))
    eastward = 1 - 2 * scalar_ref[0, 1 + cols]

    def neighbour(code, a, c):
        third = (code * 11) // 32
        row = a + third - 1
        row = jnp.where(row < 0, rows, row)
        return row * wide + 1 + c + eastward * (code - 3 * third - 1)

    low = lax.broadcasted_iota(jnp.int32, (nodes, feats // 2), 1) < feats // 4
    for a in range(rows):
        for place, c in enumerate(columns):
            b = scalar_ref[0, 1 + c]
            near = jnp.concatenate(
                [ext[neighbour(codes_ref[a, b, k], a, c)] for k in range(taps)], axis=0
            )
            weights = jnp.concatenate(
                [
                    jnp.concatenate([w_ref[q, a, place, k] for k in range(taps)], axis=1)
                    for q in range(4)
                ],
                axis=0,
            )
            derivs = jnp.dot(weights, near, preferred_element_type=F32)
            grads = [derivs[q * nodes : (q + 1) * nodes] for q in range(4)]
            now = now_ref[a, place] if number else state_ref[a, b]
            x01, x2 = coef_ref[a, b, 0], coef_ref[a, b, 1]
            rate = jnp.concatenate(tendency(now, grads, x01, x2, low), axis=1)
            out = (sum_ref[a, place] if last else state_ref[a, b]) + scale * rate
            if blend:
                blend_ref[a, place] = (1.0 / 3.0) * (
                    sum_ref[a, place] + 2.0 * now + out - state_ref[a, b]
                )
            next_ref[a, place] = out
            rounded = out.astype(BF16)
            if edge and not last:
                outs[place][a, 0] = rounded
            else:
                outs[0][a, place] = rounded
    if not last:
        if edge:
            outs[2][0, 0] = outs[0][send, 0]
            outs[2][0, 1] = outs[1][send, 0]
        else:
            outs[1][0] = outs[0][send]


def join_kernel(scalar_ref, inner_ref, edge_ref, out_ref):
    rows, cols = out_ref.shape[:2]
    for a in range(rows):
        for c in range(cols):
            source = edge_ref[a, c // (cols - 1)] if c in (0, cols - 1) else inner_ref[a, c - 1]
            out_ref[a, scalar_ref[0, 1 + c]] = source


def pick_kernel(flag, scalar_ref, first_ref, *refs):
    count = len(refs) // 2
    for i in range(count):
        refs[count + i][...] = jnp.where(
            scalar_ref[0, flag + i] == 1, first_ref[...], refs[i][...]
        )


def collect_kernel(places, *refs):
    pieces, out_ref = refs[-1 - len(places) : -1], refs[-1]
    for place, piece in zip(places, pieces):
        flat = piece.reshape(piece.shape[0] * piece.shape[1], *piece.shape[2:])
        out_ref[pl.ds(place, flat.shape[0])] = flat[...]


def ocean_kernel(
    sizes, scalar_ref, owner_ref, local_ref, interp_ref, tiles_ref, out_ref, slot_ref, buffer, sems
):
    lon_count, lat_count, rows, cols, block = sizes
    my_lon, my_lat = scalar_ref[0, 2 + cols], 1 - scalar_ref[0, 0]
    middle = lon_count // 2
    owners, local_ids = owner_ref[...], local_ref[...]
    owner_lon = owners // lat_count
    relative = (owner_lon - my_lon + (middle + 1 + lon_count)) % lon_count
    even = 1 - my_lon % 2
    towards = (relative == 2).astype(jnp.int32)
    kind = jnp.where(relative == 1, 0, 2 - (towards == even).astype(jnp.int32))
    away = (owners % lat_count != my_lat).astype(jnp.int32)
    row, col = local_ids // cols, local_ids % cols
    col = jnp.where(owner_lon % 2 == 0, cols - 1 - col, col)
    inner_count = rows * (cols - 2)
    inner_slot = (kind * 2 + away) * inner_count + row * (cols - 2) + col - 1
    edge_slot = 6 * inner_count + (relative * 2 + away) * (2 * rows)
    edge_slot += 2 * row + (col != 0).astype(jnp.int32)
    slot_ref[...] = jnp.where((col == 0) | (col == cols - 1), edge_slot, inner_slot)

    taps, tiles = slot_ref.shape
    copies = []
    for o in range(tiles):
        near = jnp.concatenate([tiles_ref[slot_ref[j, o]] for j in range(taps)], axis=0)
        buffer[o] = jnp.dot(interp_ref[o], near, preferred_element_type=F32).astype(BF16)
        if o % block == block - 1:
            part = pl.ds(o + 1 - block, block)
            copies.append(
                pltpu.make_async_copy(buffer.at[part], out_ref.at[part], sems.at[o // block])
            )
            copies[-1].start()
    for copy in copies:
        copy.wait()


def local(state, weights, positions, stencil_codes, ovl_owner, ovl_local, interp):
    rows, cols, nodes, feats = state.shape
    taps = stencil_codes.shape[-1]
    lon_count = lax.axis_size("lon")
    lat_count = lax.axis_size("lat")
    my_lon = lax.axis_index("lon")
    my_lat = lax.axis_index("lat")
    to_a = [(i, i ^ 1) for i in range(lon_count)]
    to_b = [(i, (i + 1 if i % 2 else i - 1) % lon_count) for i in range(lon_count)]
    swap = [(i, lat_count - 1 - i) for i in range(lat_count)]

    def flip(value):
        return lax.ppermute(value, "lat", swap)

    a_is_east = (my_lon % 2 == 0).astype(jnp.int32)
    order = jnp.arange(cols, dtype=jnp.int32)
    order = jnp.where(a_is_east == 1, cols - 1 - order, order)
    middle = lon_count // 2
    in_half = my_lon % middle
    turns = (in_half == middle - 2) | (in_half == 1)
    last_of_half, first_of_half = in_half == middle - 1, in_half == 0
    numbers = [1 - my_lat, *order, a_is_east, my_lon, turns, last_of_half, first_of_half]
    numbers = jnp.stack([number.astype(jnp.int32) for number in numbers])
    scalars = jnp.pad(numbers, (0, -numbers.size % 128)).reshape(1, -1)
    flags = cols + 3
    ocean_dev, intersections = ovl_local.shape
    inner_count = rows * (cols - 2)

    tile = (nodes, feats)
    inner_s = ((rows, cols - 2) + tile, BF16)
    irow_s = ((1, cols - 2) + tile, BF16)
    edge_s = ((rows, 1) + tile, BF16)
    erow_s = ((1, 2) + tile, BF16)

    own = vmem_call(
        prep_kernel,
        "prep",
        [inner_s, irow_s, edge_s, edge_s, erow_s],
        [scalars, state],
    )

    quarter = weights.shape[:2]
    coef, codes, w_inner, w_edge = pl.pallas_call(
        setup_kernel,
        out_shape=[
            pltpu.VMEM((rows, cols, 2, nodes, nodes), F32),
            pltpu.VMEM(stencil_codes.shape, jnp.int32),
            pltpu.VMEM(quarter + (cols - 2,) + weights.shape[3:], BF16),
            pltpu.VMEM(quarter + (2,) + weights.shape[3:], BF16),
        ],
        in_specs=[VMEM] + [HBM] * 3,
        out_specs=[VMEM] * 4,
        scratch_shapes=[
            pltpu.VMEM(positions.shape, F32),
            pltpu.SemaphoreType.DMA((weights.shape[0], cols)),
            pltpu.SemaphoreType.DMA((2,)),
        ],
        compiler_params=pltpu.CompilerParams(vmem_limit_bytes=4 * MIB),
        name="setup",
    )(in_vmem(scalars), in_hbm(positions), in_hbm(stencil_codes), in_hbm(weights))

    scales = (0.5 * STEP_SIZE, 0.5 * STEP_SIZE, STEP_SIZE, STEP_SIZE / 6.0)
    stages = len(scales)

    fields = {False: [], True: []}
    for number, scale in enumerate(scales):
        last = number == stages - 1
        blend = number == stages - 2
        inner, irow, edge_a, edge_b, erow = own
        halo_a = lax.ppermute(edge_a, "lon", to_a)
        halo_b = lax.ppermute(edge_b, "lon", to_b)
        near = [inner, flip(irow), edge_a, edge_b, flip(erow)]
        own = {}
        for edge in (False, True):
            if edge:
                halo_a, halo_b = lax.optimization_barrier((halo_a, halo_b, own[False][0]))[:2]
                corner_a, corner_b = flip(halo_a), flip(halo_b)
            far = [halo_a, halo_b, corner_a, corner_b] if edge else []
            field_s = ((rows, 2 if edge else cols - 2) + tile, F32)
            outs = [edge_s, edge_s, erow_s] if edge else [inner_s, irow_s]
            if last:
                outs = [((rows, 2 if edge else cols - 2) + tile, BF16)]
            outs = ([field_s] if blend else []) + [field_s] + outs
            results = vmem_call(
                functools.partial(stage_kernel, edge, number, stages, scale),
                ("edge" if edge else "inner") + ("_last" if last else ""),
                outs,
                [scalars, codes, w_edge if edge else w_inner, coef]
                + ([] if last else [state])
                + fields[edge]
                + near
                + far,
                [pltpu.VMEM(((rows + 1) * (cols + 2),) + tile, BF16)],
            )
            if blend:
                fields[edge], results = list(results[:2]), results[2:]
            else:
                fields[edge], results = (fields[edge] + [results[0]])[-2:], results[1:]
            own[edge] = results
        own = own[False] + own[True]
    next_i, next_e = fields[False][-1], fields[True][-1]
    final_i, final_e = own
    opposite = [(i, (i + middle) % lon_count) for i in range(lon_count)]
    center_i = lax.ppermute(final_i, "lon", opposite)
    center_e = lax.ppermute(final_e, "lon", opposite)

    (next_state,) = pl.pallas_call(
        join_kernel,
        out_shape=[jax.ShapeDtypeStruct(state.shape, F32)],
        in_specs=[VMEM] * 3,
        out_specs=[VMEM],
        compiler_params=pltpu.CompilerParams(vmem_limit_bytes=4 * MIB),
        name="join",
    )(scalars, next_i, next_e)
    turned_interp = pl.pallas_call(
        turn_kernel,
        out_shape=pltpu.VMEM((ocean_dev, nodes, intersections * nodes), BF16),
        in_specs=[HBM],
        out_specs=VMEM,
        scratch_shapes=[pltpu.VMEM(interp.shape, BF16), pltpu.SemaphoreType.DMA(())],
        compiler_params=pltpu.CompilerParams(vmem_limit_bytes=4 * MIB),
        name="turn_interp",
    )(in_hbm(after(interp, next_e)))


    def within_half(step):
        return [(i, i - i % middle + (i + step(i)) % middle) for i in range(lon_count)]

    up, down = within_half(lambda i: 1), within_half(lambda i: -1)
    onward = within_half(lambda i: -2 if i % 2 else 2)

    def pick(flag, *pieces):
        return vmem_call(
            functools.partial(pick_kernel, flag),
            "pick",
            [(pieces[0].shape, BF16)] * (len(pieces) - 1),
            [scalars, *pieces],
        )

    def collect(tiles, place, pieces):
        size = pieces[0].shape[0] * pieces[0].shape[1]
        return vmem_call(
            functools.partial(collect_kernel, [place + i * size for i in range(len(pieces))]),
            "collect",
            [((6 * rows * cols,) + tile, BF16)],
            ([] if tiles is None else [tiles]) + pieces,
            aliases=None if tiles is None else {0: 0},
        )[0]

    native = lax.ppermute(final_i, "lon", to_a)
    paired = lax.ppermute(after(center_i, native, next_state, turned_interp), "lon", to_a)
    passed = lax.ppermute(pick(flags, native, paired)[0], "lon", onward)
    tiles = collect(
        None, 0, [center_i, flip(center_i), paired, flip(paired), passed, flip(passed)]
    )
    going_up, going_down = pick(flags + 1, final_e, center_e, center_e)
    below = lax.ppermute(going_up, "lon", up)
    above = lax.ppermute(going_down, "lon", down)
    tiles = collect(
        tiles,
        6 * inner_count,
        [below, flip(below), center_e, flip(center_e), above, flip(above)],
    )
    block = 4
    ocean = pl.pallas_call(
        functools.partial(ocean_kernel, (lon_count, lat_count, rows, cols, block)),
        out_shape=pltpu.HBM((ocean_dev, nodes, feats), BF16),
        in_specs=[VMEM] * 5,
        out_specs=HBM,
        scratch_shapes=[
            pltpu.VMEM((intersections, ocean_dev), jnp.int32),
            pltpu.VMEM((ocean_dev, nodes, feats), BF16),
            pltpu.SemaphoreType.DMA((ocean_dev // block,)),
        ],
        compiler_params=pltpu.CompilerParams(vmem_limit_bytes=6 * MIB),
        name="ocean",
    )(
        *[
            in_vmem(array)
            for array in (scalars, ovl_owner[:, :, 0].T, ovl_local.T, turned_interp, tiles)
        ]
    )
    return next_state, ocean


def solution(mesh):
    placed = (
        P(("member", "lat"), "lon", None, None),
        P(None, "lat", "lon", None, None, None),
        P(None, "lat", "lon", None),
        P("lat", "lon", None),
        P(("lon", "lat"), None, None),
        P(("lon", "lat"), None),
        P(("lon", "lat"), None, None, None),
    )
    return jax.shard_map(
        local,
        mesh=mesh,
        in_specs=placed,
        out_specs=(
            P(("member", "lat"), "lon", None, None),
            P(("member", "lon", "lat"), None, None),
        ),
        check_vma=False,
    )
```

```python
import functools

import jax
import jax.numpy as jnp
from jax import lax
from jax.experimental import pallas as pl
from jax.experimental.pallas import tpu as pltpu
from jax.sharding import PartitionSpec as P

CORIOLIS = 2.0
STEP_SIZE = 0.2
BF16 = jnp.bfloat16
F32 = jnp.float32
VMEM = pl.BlockSpec(memory_space=pltpu.VMEM)
HBM = pl.BlockSpec(memory_space=pltpu.HBM)
MIB = 1024 * 1024


def in_vmem(value):
    return pltpu.with_memory_space_constraint(value, pltpu.VMEM)


def in_hbm(value):
    return pltpu.with_memory_space_constraint(value, pltpu.HBM)


def vmem_call(kernel, name, outs, arrays, scratch=(), limit=4, aliases=None):
    return pl.pallas_call(
        kernel,
        out_shape=[pltpu.VMEM(shape, dtype) for shape, dtype in outs],
        in_specs=[VMEM] * len(arrays),
        out_specs=[VMEM] * len(outs),
        scratch_shapes=list(scratch),
        compiler_params=pltpu.CompilerParams(vmem_limit_bytes=limit * MIB),
        cost_estimate=pl.CostEstimate(flops=1000, bytes_accessed=1000, transcendentals=0),
        input_output_aliases=aliases or {},
        name=name,
    )(*[in_vmem(array) for array in arrays])


def after(value, *others):
    return lax.optimization_barrier((value,) + others)[0]


def prep_kernel(scalar_ref, state_ref, inner_ref, irow_ref, edge_a_ref, edge_b_ref, erow_ref):
    rows, cols = state_ref.shape[:2]
    for a in range(rows):
        edge_a_ref[a, 0] = state_ref[a, scalar_ref[0, 1]].astype(BF16)
        edge_b_ref[a, 0] = state_ref[a, scalar_ref[0, cols]].astype(BF16)
        for c in range(1, cols - 1):
            inner_ref[a, c - 1] = state_ref[a, scalar_ref[0, 1 + c]].astype(BF16)
    send = scalar_ref[0, 0]
    irow_ref[0] = inner_ref[send]
    erow_ref[0, 0] = edge_a_ref[send, 0]
    erow_ref[0, 1] = edge_b_ref[send, 0]


def setup_kernel(
    scalar_ref, pos_hbm, codes_hbm, w_ref, coef_ref, index_ref, inner_ref, edge_ref, pos_ref, codes_ref, sems, small_sems
):
    small = [
        pltpu.make_async_copy(pos_hbm, pos_ref, small_sems.at[0]),
        pltpu.make_async_copy(codes_hbm, codes_ref, small_sems.at[1]),
    ]
    for copy in small:
        copy.start()
    rows, cols, nodes = pos_ref.shape[1:]
    copies = []
    for c in range(cols):
        on_edge = c in (0, cols - 1)
        target, place = (edge_ref, min(c, 1)) if on_edge else (inner_ref, c - 1)
        for q in range(w_ref.shape[0]):
            copies.append(
                pltpu.make_async_copy(
                    w_ref.at[q, :, pl.ds(scalar_ref[0, 1 + c], 1)],
                    target.at[q, :, pl.ds(place, 1)],
                    sems.at[q, c],
                )
            )
    for copy in copies:
        copy.start()
    for copy in small:
        copy.wait()
    codes = codes_ref[...]
    third = (codes * 11) // 32
    row = lax.broadcasted_iota(jnp.int32, codes.shape, 0) + third - 1
    row = jnp.where(row < 0, rows, row)
    col = lax.broadcasted_iota(jnp.int32, codes.shape, 1) + codes - 3 * third - 1
    col = jnp.where(scalar_ref[0, 1 + cols] == 1, cols - 1 - col, col)
    index_ref[...] = row * (cols + 2) + 1 + col
    low = lax.broadcasted_iota(jnp.int32, (nodes, nodes), 1) < nodes // 2
    for a in range(rows):
        for b in range(cols):
            x0, x1, x2 = (
                jnp.broadcast_to(pos_ref[c, a, b][None, :], (nodes, nodes)).T for c in range(3)
            )
            coef_ref[a, b, 0] = jnp.where(low, x0, x1)
            coef_ref[a, b, 1] = x2
    for copy in copies:
        copy.wait()


def turn_kernel(interp_ref, turned_ref, interp, sem):
    copy = pltpu.make_async_copy(interp_ref, interp, sem)
    copy.start()
    copy.wait()
    tiles, taps, nodes, points = interp.shape
    for o in range(tiles):
        turned_ref[o] = interp[o].reshape(taps * nodes, points).T


def turned(value):
    return pltpu.roll(value, value.shape[-1] // 2, axis=1)


def tendency(tile, grads, x01, x2, low):
    half = tile.shape[-1] // 2
    sa, sb = tile[:, :half], tile[:, half:]
    ra, rb = turned(sa), turned(sb)
    v0 = jnp.where(low, sa, ra)
    v1 = jnp.where(low, ra, sa)
    v2 = jnp.where(low, sb, rb)
    ga = [g[:, :half] for g in grads]
    gb = [g[:, half:] for g in grads]
    t0a, t0b, t2b = turned(ga[0]), turned(gb[0]), turned(gb[2])
    x10 = turned(x01)
    spin = CORIOLIS * x2
    cross = spin * (x10 * v2 - x2 * ra)
    fa = (
        ga[3]
        - (v0 * ga[0] + v1 * ga[1] + v2 * ga[2])
        - jnp.where(low, cross + t0b, gb[1] - cross)
    )
    spread = sb * (t0a + ga[1] + t2b)
    fb = (
        gb[3]
        - (v0 * gb[0] + v1 * gb[1] + v2 * gb[2])
        - jnp.where(low, spin * (x01 * v1 - x10 * v0) + t2b, spread)
    )
    x2_low = jnp.where(low, x2, 0.0)
    part = x01 * fa + x2_low * fb
    radial = part + turned(part)
    return fa - x01 * radial, fb - x2_low * radial


def stage_kernel(edge, number, stages, scale, scalar_ref, index_ref, w_ref, coef_ref, *refs):
    refs = list(refs)
    ext = refs.pop()
    rows, cols = coef_ref.shape[:2]
    nodes, feats = ext.shape[1:]
    taps = w_ref.shape[3]
    wide = cols + 2
    last = number == stages - 1
    blend = number == stages - 2
    state_ref = None if last else refs.pop(0)
    sum_ref = refs.pop(0) if last or blend else None
    now_ref = refs.pop(0) if number else None
    inner_ref, irow_ref, edge_a_ref, edge_b_ref, erow_ref = refs[:5]
    refs = refs[5:]
    send = scalar_ref[0, 0]
    for a in range(rows):
        ext[a * wide + 1] = edge_a_ref[a, 0]
        ext[a * wide + cols] = edge_b_ref[a, 0]
        ext[pl.ds(a * wide + 2, cols - 2)] = inner_ref[a]
    ext[rows * wide + 1] = erow_ref[0, 0]
    ext[rows * wide + cols] = erow_ref[0, 1]
    ext[pl.ds(rows * wide + 2, cols - 2)] = irow_ref[0]
    if edge:
        halo_a_ref, halo_b_ref, corner_a_ref, corner_b_ref = refs[:4]
        refs = refs[4:]
        for a in range(rows):
            ext[a * wide] = halo_a_ref[a, 0]
            ext[a * wide + cols + 1] = halo_b_ref[a, 0]
        ext[rows * wide] = corner_a_ref[1 - send, 0]
        ext[rows * wide + cols + 1] = corner_b_ref[1 - send, 0]
    blend_ref = refs.pop(0) if blend else None
    next_ref, *outs = refs
    columns = (0, cols - 1) if edge else tuple(range(1, cols - 1))
    low = lax.broadcasted_iota(jnp.int32, (nodes, feats // 2), 1) < feats // 4
    for a in range(rows):
        for place, c in enumerate(columns):
            b = scalar_ref[0, 1 + c]
            near = jnp.concatenate(
                [ext[index_ref[a, b, k]] for k in range(taps)], axis=0
            )
            weights = jnp.concatenate(
                [
                    jnp.concatenate([w_ref[q, a, place, k] for k in range(taps)], axis=1)
                    for q in range(4)
                ],
                axis=0,
            )
            derivs = jnp.dot(weights, near, preferred_element_type=F32)
            grads = [derivs[q * nodes : (q + 1) * nodes] for q in range(4)]
            now = now_ref[a, place] if number else state_ref[a, b]
            x01, x2 = coef_ref[a, b, 0], coef_ref[a, b, 1]
            rate = jnp.concatenate(tendency(now, grads, x01, x2, low), axis=1)
            out = (sum_ref[a, place] if last else state_ref[a, b]) + scale * rate
            if blend:
                blend_ref[a, place] = (1.0 / 3.0) * (
                    sum_ref[a, place] + 2.0 * now + out - state_ref[a, b]
                )
            next_ref[a, place] = out
            rounded = out.astype(BF16)
            if edge:
                outs[place][a, 0] = rounded
            else:
                outs[0][a, place] = rounded
    if not last:
        if edge:
            outs[2][0, 0] = outs[0][send, 0]
            outs[2][0, 1] = outs[1][send, 0]
        else:
            outs[1][0] = outs[0][send]


def join_kernel(scalar_ref, inner_ref, edge_ref, out_ref):
    rows, cols = out_ref.shape[:2]
    for a in range(rows):
        for c in range(cols):
            source = edge_ref[a, c // (cols - 1)] if c in (0, cols - 1) else inner_ref[a, c - 1]
            out_ref[a, scalar_ref[0, 1 + c]] = source


def pick_kernel(flag, scalar_ref, first_ref, *refs):
    count = len(refs) // 2
    for i in range(count):
        refs[count + i][...] = jnp.where(
            scalar_ref[0, flag + i] == 1, first_ref[...], refs[i][...]
        )


def collect_kernel(places, *refs):
    pieces, out_ref = refs[-1 - len(places) : -1], refs[-1]
    for place, piece in zip(places, pieces):
        flat = piece.reshape(-1, *piece.shape[-2:])
        out_ref[pl.ds(place, flat.shape[0])] = flat[...]


def ocean_kernel(
    sizes, scalar_ref, owner_ref, local_ref, interp_ref, tiles_ref, out_ref, slot_ref, buffer, sems
):
    lon_count, lat_count, rows, cols, block = sizes
    my_lon, my_lat = scalar_ref[0, 2 + cols], 1 - scalar_ref[0, 0]
    middle = lon_count // 2
    owners, local_ids = owner_ref[...], local_ref[...]
    owner_lon = owners // lat_count
    relative = (owner_lon - my_lon + (middle + 1 + lon_count)) % lon_count
    even = 1 - my_lon % 2
    towards = (relative == 2).astype(jnp.int32)
    kind = jnp.where(relative == 1, 0, 2 - (towards == even).astype(jnp.int32))
    away = (owners % lat_count != my_lat).astype(jnp.int32)
    row, col = local_ids // cols, local_ids % cols
    col = jnp.where(owner_lon % 2 == 0, cols - 1 - col, col)
    inner_count = rows * (cols - 2)
    early, late = 2 * inner_count + 2 * rows, inner_count + 4 * rows
    place = row * (cols - 2) + col - 1
    on_far_edge = (col != 0).astype(jnp.int32)
    edge_early = 2 * inner_count + on_far_edge * rows + row
    edge_late = inner_count + (2 * on_far_edge + (relative == 2).astype(jnp.int32)) * rows + row
    on_edge = (col == 0) | (col == cols - 1)
    is_late = jnp.where(on_edge, (relative != 1).astype(jnp.int32), (kind == 2).astype(jnp.int32))
    early_slot = jnp.where(on_edge, edge_early, kind * inner_count + place) + away * early
    late_slot = jnp.where(on_edge, edge_late, place) + 2 * early + away * late
    slot_ref[...] = jnp.where(is_late == 1, late_slot, early_slot)

    taps, tiles = slot_ref.shape
    copies = []
    for o in range(tiles):
        near = jnp.concatenate([tiles_ref[slot_ref[j, o]] for j in range(taps)], axis=0)
        buffer[o] = jnp.dot(interp_ref[o], near, preferred_element_type=F32).astype(BF16)
        if o % block == block - 1:
            part = pl.ds(o + 1 - block, block)
            copies.append(
                pltpu.make_async_copy(buffer.at[part], out_ref.at[part], sems.at[o // block])
            )
            copies[-1].start()
    for copy in copies:
        copy.wait()


def local(state, weights, positions, stencil_codes, ovl_owner, ovl_local, interp):
    rows, cols, nodes, feats = state.shape
    taps = stencil_codes.shape[-1]
    lon_count = lax.axis_size("lon")
    lat_count = lax.axis_size("lat")
    my_lon = lax.axis_index("lon")
    my_lat = lax.axis_index("lat")
    to_a = [(i, i ^ 1) for i in range(lon_count)]
    to_b = [(i, (i + 1 if i % 2 else i - 1) % lon_count) for i in range(lon_count)]
    swap = [(i, lat_count - 1 - i) for i in range(lat_count)]

    def flip(value):
        return lax.ppermute(value, "lat", swap)

    a_is_east = (my_lon % 2 == 0).astype(jnp.int32)
    order = jnp.arange(cols, dtype=jnp.int32)
    order = jnp.where(a_is_east == 1, cols - 1 - order, order)
    middle = lon_count // 2
    in_half = my_lon % middle
    turns = (in_half == middle - 2) | (in_half == 1)
    last_of_half, first_of_half = in_half == middle - 1, in_half == 0
    numbers = [1 - my_lat, *order, a_is_east, my_lon, turns, last_of_half, first_of_half]
    numbers = jnp.stack([number.astype(jnp.int32) for number in numbers])
    scalars = jnp.pad(numbers, (0, -numbers.size % 128)).reshape(1, -1)
    flags = cols + 3
    ocean_dev, intersections = ovl_local.shape
    inner_count = rows * (cols - 2)

    tile = (nodes, feats)
    inner_s = ((rows, cols - 2) + tile, BF16)
    irow_s = ((1, cols - 2) + tile, BF16)
    edge_s = ((rows, 1) + tile, BF16)
    erow_s = ((1, 2) + tile, BF16)

    inner, irow, *edges = vmem_call(
        prep_kernel,
        "prep",
        [inner_s, irow_s, edge_s, edge_s, erow_s],
        [scalars, state],
    )
    own = [inner, flip(irow), *edges]

    quarter = weights.shape[:2]
    coef, index, w_inner, w_edge = pl.pallas_call(
        setup_kernel,
        out_shape=[
            pltpu.VMEM((rows, cols, 2, nodes, nodes), F32),
            pltpu.VMEM(stencil_codes.shape, jnp.int32),
            pltpu.VMEM(quarter + (cols - 2,) + weights.shape[3:], BF16),
            pltpu.VMEM(quarter + (2,) + weights.shape[3:], BF16),
        ],
        in_specs=[VMEM] + [HBM] * 3,
        out_specs=[VMEM] * 4,
        scratch_shapes=[
            pltpu.VMEM(positions.shape, F32),
            pltpu.VMEM(stencil_codes.shape, jnp.int32),
            pltpu.SemaphoreType.DMA((weights.shape[0], cols)),
            pltpu.SemaphoreType.DMA((2,)),
        ],
        compiler_params=pltpu.CompilerParams(vmem_limit_bytes=4 * MIB),
        name="setup",
    )(in_vmem(scalars), in_hbm(positions), in_hbm(stencil_codes), in_hbm(weights))

    scales = (0.5 * STEP_SIZE, 0.5 * STEP_SIZE, STEP_SIZE, STEP_SIZE / 6.0)
    stages = len(scales)

    fields = {False: [], True: []}
    for number, scale in enumerate(scales):
        last = number == stages - 1
        blend = number == stages - 2
        inner, irow, edge_a, edge_b, erow = own
        halo_a = lax.ppermute(edge_a, "lon", to_a)
        halo_b = lax.ppermute(edge_b, "lon", to_b)
        near = [inner, irow, edge_a, edge_b, flip(erow)]
        own = {}
        for edge in (False, True):
            if edge:
                ahead = own[False]
                if not last:
                    ahead[1] = flip(ahead[1])
                ahead = ahead if number else ahead[:1]
                halo_a, halo_b = lax.optimization_barrier((halo_a, halo_b, *ahead))[:2]
                corner_a, corner_b = flip(halo_a), flip(halo_b)
            far = [halo_a, halo_b, corner_a, corner_b] if edge else []
            field_s = ((rows, 2 if edge else cols - 2) + tile, F32)
            outs = [edge_s, edge_s, erow_s] if edge else [inner_s, irow_s]
            outs = ([field_s] if blend else []) + [field_s] + (outs[:-1] if last else outs)
            results = vmem_call(
                functools.partial(stage_kernel, edge, number, stages, scale),
                ("edge" if edge else "inner") + ("_last" if last else ""),
                outs,
                [scalars, index, w_edge if edge else w_inner, coef]
                + ([] if last else [state])
                + fields[edge]
                + near
                + far,
                [pltpu.VMEM(((rows + 1) * (cols + 2),) + tile, BF16)],
            )
            if blend:
                fields[edge], results = list(results[:2]), results[2:]
            else:
                fields[edge], results = (fields[edge] + [results[0]])[-2:], results[1:]
            own[edge] = list(results)
        own = own[False] + own[True]
    next_i, next_e = fields[False][-1], fields[True][-1]
    final_i, final_a, final_b = own
    opposite = [(i, (i + middle) % lon_count) for i in range(lon_count)]
    center_i = lax.ppermute(final_i, "lon", opposite)

    (next_state,) = pl.pallas_call(
        join_kernel,
        out_shape=[jax.ShapeDtypeStruct(state.shape, F32)],
        in_specs=[VMEM] * 3,
        out_specs=[VMEM],
        compiler_params=pltpu.CompilerParams(vmem_limit_bytes=4 * MIB),
        name="join",
    )(scalars, next_i, next_e)
    turned_interp = pl.pallas_call(
        turn_kernel,
        out_shape=pltpu.VMEM((ocean_dev, nodes, intersections * nodes), BF16),
        in_specs=[HBM],
        out_specs=VMEM,
        scratch_shapes=[pltpu.VMEM(interp.shape, BF16), pltpu.SemaphoreType.DMA(())],
        compiler_params=pltpu.CompilerParams(vmem_limit_bytes=4 * MIB),
        name="turn_interp",
    )(in_hbm(after(interp, next_e)))


    def within_half(step):
        return [(i, i - i % middle + (i + step(i)) % middle) for i in range(lon_count)]

    up, down = within_half(lambda i: 1), within_half(lambda i: -1)
    onward = within_half(lambda i: -2 if i % 2 else 2)

    def pick(flag, *pieces):
        return vmem_call(
            functools.partial(pick_kernel, flag),
            "pick",
            [(pieces[0].shape, BF16)] * (len(pieces) - 1),
            [scalars, *pieces],
        )

    def collect(name, size, pieces, tiles=None, place=0):
        places = [place + sum(counted(piece) for piece in pieces[:i]) for i in range(len(pieces))]
        return vmem_call(
            functools.partial(collect_kernel, places),
            name,
            [((size,) + tile, BF16)],
            ([] if tiles is None else [tiles]) + pieces,
            aliases=None if tiles is None else {0: 0},
        )[0]

    def counted(piece):
        return piece.size // (nodes * feats)

    native = lax.ppermute(final_i, "lon", to_a)
    paired = lax.ppermute(after(center_i, native, next_state, turned_interp), "lon", to_a)
    center_a = lax.ppermute(final_a, "lon", opposite)
    center_b = lax.ppermute(after(final_b, paired), "lon", opposite)
    passed = lax.ppermute(pick(flags, native, paired)[0], "lon", onward)
    late = [passed]
    for final, center in ((final_a, center_a), (final_b, center_b)):
        going_up, going_down = pick(flags + 1, final, center, center)
        late += [lax.ppermute(going_up, "lon", up), lax.ppermute(going_down, "lon", down)]
    early_size, late_size = 2 * inner_count + 2 * rows, inner_count + 4 * rows
    size = 2 * (early_size + late_size)
    early = collect("early", early_size, [center_i, paired, center_a, center_b])
    late = collect("late", late_size, late)
    tiles = collect("gather", size, [early, flip(early), late])
    tiles = collect("gather", size, [flip(late)], tiles, size - late_size)
    block = 4
    ocean = pl.pallas_call(
        functools.partial(ocean_kernel, (lon_count, lat_count, rows, cols, block)),
        out_shape=pltpu.HBM((ocean_dev, nodes, feats), BF16),
        in_specs=[VMEM] * 5,
        out_specs=HBM,
        scratch_shapes=[
            pltpu.VMEM((intersections, ocean_dev), jnp.int32),
            pltpu.VMEM((ocean_dev, nodes, feats), BF16),
            pltpu.SemaphoreType.DMA((ocean_dev // block,)),
        ],
        compiler_params=pltpu.CompilerParams(vmem_limit_bytes=6 * MIB),
        name="ocean",
    )(
        *[
            in_vmem(array)
            for array in (scalars, ovl_owner[:, :, 0].T, ovl_local.T, turned_interp, tiles)
        ]
    )
    return next_state, ocean


def solution(mesh):
    placed = (
        P(("member", "lat"), "lon", None, None),
        P(None, "lat", "lon", None, None, None),
        P(None, "lat", "lon", None),
        P("lat", "lon", None),
        P(("lon", "lat"), None, None),
        P(("lon", "lat"), None),
        P(("lon", "lat"), None, None, None),
    )
    return jax.shard_map(
        local,
        mesh=mesh,
        in_specs=placed,
        out_specs=(
            P(("member", "lat"), "lon", None, None),
            P(("member", "lon", "lat"), None, None),
        ),
        check_vma=False,
    )
```
